512 devices in a mesh: bcast: 32 (over x_lo, z, core), grad: 16 (over x_hi, y).
Axes of the slice: x: 4 (x_hi: 2, x_lo: 2; x = x_hi * 2 + x_lo), y: 8, z: 8, core: 2. Of those that a mesh axis runs over, the one named last changes fastest.
Arguments:
- activations: bfloat16 [32768, 16, 1024], P('bcast', 'grad'), may hold values from -150 to 150
- gradient: bfloat16 [6144, 16, 1024], P(('bcast', 'grad')), may hold values from -6 to 6
- block_map: int32 [16], replicated, may hold values from 0 to 15, each once
Outputs:
- precond: bfloat16 [6144, 16, 1024], P('bcast', 'grad')
The draws below stay inside these ranges and needn't reach their ends.
Inputs may be any that keep to these rules, and one draw needn't show every extreme that they name: `block_map`: each factor block appears exactly once.
All inputs are finite; a program needn't handle non-finite values.
Results may differ from the reference program's by a relative error of at most 0.0066.
Values may be sent and summed in bfloat16 or wider, within the bound.
A program may use at most 128 MiB of HBM per device.

```python
import math
import jax
import jax.numpy as jnp
from jax import lax

DOUT = 6144
BS = 1024
KB = 16
TOKENS = 32768


def draw_activations(key, part):
    key = jax.random.fold_in(key, 11)
    key_noise, key_common, key_load, key_scale = jax.random.split(key, 4)
    shape = (TOKENS, KB, BS)
    noise = jax.random.normal(key_noise, shape, jnp.float32)
    scale_lo, scale_hi, common_weight = (0.5, 3.0, 0.8)
    common = jax.random.normal(key_common, (TOKENS, KB, 1), jnp.float32)
    loading = jax.random.uniform(key_load, (1, KB, BS), jnp.float32, -1.0, 1.0)
    feature_scale = jnp.exp(jax.random.uniform(key_scale, (1, KB, BS), jnp.float32, math.log(scale_lo), math.log(scale_hi)))
    position = jnp.arange(TOKENS, dtype=jnp.float32)
    token_scale = jnp.sqrt(1.0 + 2.0 * position / max(TOKENS - 1, 1))
    mixed = noise + 0.7 * jnp.roll(noise, 1, axis=2) + common_weight * common * loading
    return (token_scale[:, None, None] * feature_scale * mixed).astype(jnp.bfloat16)


def level_of(stream_key, extent, cuts, smallest, top_value):
    level, own = 1.0, jax.random.fold_in(stream_key, 6)
    for dim, shards_of in cuts:
        heights = jnp.exp(jax.random.uniform(jax.random.fold_in(own, dim), (shards_of,), jnp.float32, smallest / len(cuts), top_value / len(cuts)))
        level = level * jnp.repeat(heights, extent[dim] // shards_of).reshape([-1 if axis == dim else 1 for axis in range(len(extent))])
    return level


def bell_draw(key, dims, deviation, most, pieces=(), kind=jnp.bfloat16):
    array = jax.random.normal(key, dims, jnp.float32) * deviation
    if len(pieces) > 0:
        array = level_of(key, dims, pieces, -0.22, 0.18) * array
    return jnp.clip(array, min=-most, max=most).astype(kind)


def setup_inputs(seed: int = 0) -> dict:
    key_list = jax.random.split(jax.random.key(seed), 4)
    return {
        "activations": draw_activations(jax.random.fold_in(key_list[3], 71), 0),
        "gradient": bell_draw(key_list[1], (DOUT, KB, BS), 1.0, 6.0, ((0, 512),)),
        "block_map": jax.random.permutation(key_list[2], KB).astype(jnp.int32),
    }


def inverse_root(covariance):
    identity = jnp.eye(covariance.shape[0], dtype=jnp.float32)
    lower_factor = jnp.linalg.cholesky(covariance)
    return jax.scipy.linalg.solve_triangular(lower_factor, identity, lower=True).astype(jnp.bfloat16)

def reference(activations, gradient, block_map):
    token_count = activations.shape[0]
    width = activations.shape[2]
    identity = jnp.eye(width, dtype=jnp.float32)

    def one_block(block_index):
        act_rows = lax.dynamic_index_in_dim(activations, block_index, 1, keepdims=False)
        covariance = lax.dot_general(act_rows.astype(jnp.float32), act_rows.astype(jnp.float32), (((0,), (0,)), ((), ())), preferred_element_type=jnp.float32) / token_count + identity
        root_factor = inverse_root(covariance)
        chooser = (block_map == block_index).astype(jnp.float32)
        grad_tile = jnp.einsum('rjb,j->rb', gradient.astype(jnp.float32), chooser).astype(jnp.bfloat16)
        half_done = lax.dot_general(grad_tile.astype(jnp.float32), root_factor.astype(jnp.float32), (((1,), (1,)), ((), ())), preferred_element_type=jnp.float32).astype(jnp.bfloat16)
        return jnp.dot(half_done.astype(jnp.float32), root_factor.astype(jnp.float32), preferred_element_type=jnp.float32).astype(jnp.bfloat16)
    stacked = lax.map(one_block, jnp.arange(KB, dtype=jnp.int32))
    return jnp.transpose(stacked, (1, 0, 2))
```

```python
import functools

import jax
import jax.numpy as jnp
from jax import lax
from jax.experimental import pallas as pl
from jax.experimental.pallas import tpu as pltpu
from jax.sharding import PartitionSpec as P

MESH = pl.DeviceIdType.MESH
F32, BF16 = jnp.float32, jnp.bfloat16
B = 128


def block_rows(i, j):
    return (j * 8 - j * (j - 1) // 2 + (i - j)) * B


def covariance_kernel(act_ref, out_ref):
    for j in range(8):
        column = act_ref[:, j * B : (j + 1) * B]
        part = lax.dot_general(
            act_ref[:, j * B :], column, (((0,), (0,)), ((), ())), preferred_element_type=F32
        )
        out_ref[pl.ds(block_rows(j, j), (8 - j) * B), :] = part


def exchange_kernel(part_ref, grad_ref, sum_ref, tile_ref, acc, from_core, plus, minus, from_x,
                    core_s, core_r, plus_s, plus_r, minus_s, minus_r, x_s, x_r,
                    gx_s, gx_r, gp_s, gp_r, gm_s, gm_r, gc_s, gc_r, grad_s, grad_r, own_sem):
    HALF, CHUNK, SUB = 2304, 288, 144
    me = lax.axis_index("bcast")
    column = lax.axis_index("grad")
    core, z, x = me % 2, (me // 2) % 8, me // 16
    at = lambda c, zz, xx: {"bcast": xx * 16 + (zz % 8) * 2 + c}
    twin, up, down, across = at(1 - core, z, x), at(core, z + 1, x), at(core, z + 7, x), at(core, z, 1 - x)

    barrier = pltpu.get_barrier_semaphore()
    for peer in (twin, up, down, across):
        pl.semaphore_signal(barrier, inc=1, device_id=peer, device_id_type=MESH)
    for d in range(1, 16):
        pl.semaphore_signal(barrier, inc=1, device_id={"grad": (column + d) % 16}, device_id_type=MESH)
    pl.semaphore_wait(barrier, 19)

    def send(src, dst, s, r, to):
        c = pltpu.make_async_remote_copy(src_ref=src, dst_ref=dst, send_sem=s, recv_sem=r,
                                         device_id=to, device_id_type=MESH)
        c.start()
        return c

    def rows(q, h=None):
        if h is None:
            return pl.ds((q % 8) * CHUNK, CHUNK)
        return pl.ds((q % 8) * CHUNK + h * SUB, SUB)

    def half_rows(c, q, h=None):
        if h is None:
            return pl.ds(c * HALF + (q % 8) * CHUNK, CHUNK)
        return pl.ds(c * HALF + (q % 8) * CHUNK + h * SUB, SUB)

    order = [4, 5, 3, 6, 2, 7, 1, 0]
    waits = []
    cores = {}
    for n, d in enumerate(order):
        cores[d] = send(part_ref.at[half_rows(1 - core, z + d)], from_core.at[rows(z + d)],
                        core_s.at[n], core_r.at[n], twin)
    tiles = []
    for d in range(1, 16):
        to = (column + d) % 16
        tiles.append(send(grad_ref.at[to], tile_ref.at[column], grad_s.at[d], grad_r.at[d], {"grad": to}))
    own = pltpu.make_async_copy(grad_ref.at[column], tile_ref.at[column], own_sem)
    own.start()

    for n, d in enumerate(order):
        cores[d].wait_recv()
        acc[rows(z + d)] = part_ref[half_rows(core, z + d)] + from_core[rows(z + d)]
        if d == 4:
            p = [send(acc.at[rows(z + 4, h)], plus.at[0, h], plus_s.at[0, h], plus_r.at[0, h], up) for h in (0, 1)]
            waits += p
        if d == 5:
            m = [send(acc.at[rows(z + 5, h)], minus.at[0, h], minus_s.at[0, h], minus_r.at[0, h], down) for h in (0, 1)]
            waits += m
    for s in range(1, 4):
        q = []
        for h in (0, 1):
            p[h].wait_recv()
            acc[rows(z + 4 - s, h)] += plus[s - 1, h]
            q.append(send(acc.at[rows(z + 4 - s, h)], plus.at[s, h], plus_s.at[s, h], plus_r.at[s, h], up))
        p = q
        waits += q
        if s < 3:
            q = []
            for h in (0, 1):
                m[h].wait_recv()
                acc[rows(z + 5 + s, h)] += minus[s - 1, h]
                q.append(send(acc.at[rows(z + 5 + s, h)], minus.at[s, h], minus_s.at[s, h], minus_r.at[s, h], down))
            m = q
            waits += q
    for h in (0, 1):
        m[h].wait_recv()
        acc[rows(z, h)] += minus[2, h]
    for h in (0, 1):
        p[h].wait_recv()
        acc[rows(z, h)] += plus[3, h]
    cx = send(acc.at[rows(z, 1 - x)], from_x, x_s, x_r, across)
    cx.wait_recv()
    mine = half_rows(core, z, x)
    sum_ref[mine] = acc[rows(z, x)] + from_x[...]
    waits.append(cx)
    gx = send(sum_ref.at[mine], sum_ref.at[mine], gx_s, gx_r, across)
    waits.append(gx)
    def chunk_send(q, h, sem_s, sem_r, k, hh, to):
        r = half_rows(core, q, h)
        return send(sum_ref.at[r], sum_ref.at[r], sem_s.at[k, hh], sem_r.at[k, hh], to)
    P0, M0 = [None, None], [None, None]
    for k, h in ((0, x), (1, 1 - x)):
        if k == 1:
            gx.wait_recv()
        P0[k] = chunk_send(z, h, gp_s, gp_r, 0, k, up)
        M0[k] = chunk_send(z, h, gm_s, gm_r, 0, k, down)
    waits += P0 + M0
    fin = []
    r = half_rows(core, z)
    fin.append(send(sum_ref.at[r], sum_ref.at[r], gc_s.at[0], gc_r.at[0], twin))
    for s in range(1, 5):
        Q = []
        for k, h in ((0, x), (1, 1 - x)):
            P0[k].wait_recv()
            if s < 4:
                Q.append(chunk_send(z - s + 8, h, gp_s, gp_r, s, k, up))
        P0 = Q
        waits += Q
        r = half_rows(core, z - s + 8)
        fin.append(send(sum_ref.at[r], sum_ref.at[r], gc_s.at[s], gc_r.at[s], twin))
        if s < 4:
            Q = []
            for k, h in ((0, x), (1, 1 - x)):
                M0[k].wait_recv()
                if s < 3:
                    Q.append(chunk_send(z + s, h, gm_s, gm_r, s, k, down))
            M0 = Q
            waits += Q
            r = half_rows(core, z + s)
            fin.append(send(sum_ref.at[r], sum_ref.at[r], gc_s.at[4 + s], gc_r.at[4 + s], twin))
    for c in fin:
        c.wait()
    for c in waits:
        c.wait_send()
    for d in range(8):
        cores[order[d]].wait_send()
    for c in tiles:
        c.wait()
    own.wait()


def exchange(part, grads):
    dma = pltpu.SemaphoreType.DMA
    vm = pl.BlockSpec(memory_space=pltpu.VMEM)
    return pl.pallas_call(
        exchange_kernel,
        out_shape=(jax.ShapeDtypeStruct((4608, B), F32), jax.ShapeDtypeStruct(grads.shape, BF16)),
        in_specs=[vm, vm],
        out_specs=(vm, vm),
        scratch_shapes=[
            pltpu.VMEM((2304, B), F32), pltpu.VMEM((2304, B), F32),
            pltpu.VMEM((4, 2, 144, B), F32), pltpu.VMEM((3, 2, 144, B), F32), pltpu.VMEM((144, B), F32),
            dma((8,)), dma((8,)), dma((4, 2)), dma((4, 2)), dma((3, 2)), dma((3, 2)), dma, dma,
            dma, dma, dma((4, 2)), dma((4, 2)), dma((3, 2)), dma((3, 2)), dma((8,)), dma((8,)),
            dma((16,)), dma((16,)), dma,
        ],
        compiler_params=pltpu.CompilerParams(collective_id=0, has_side_effects=True, vmem_limit_bytes=48 << 20),
    )(part, grads)


def covariance(act):
    vm = pl.BlockSpec(memory_space=pltpu.VMEM)
    return pl.pallas_call(
        covariance_kernel,
        out_shape=jax.ShapeDtypeStruct((4608, B), F32),
        in_specs=[vm], out_specs=vm,
        compiler_params=pltpu.CompilerParams(vmem_limit_bytes=48 << 20),
    )(act)


def lb(t,j): return jnp.broadcast_to(t[:,j:j+1],(8,128))
def sb(t,r): return jnp.broadcast_to(t[r:r+1,:],(8,128))
def tsum(xs):
    xs=list(xs)
    while len(xs)>1:
        xs=[xs[i]+xs[i+1] if i+1<len(xs) else xs[i] for i in range(0,len(xs),2)]
    return xs[0]
def split(x):
    h=x.astype(BF16); r=x-h.astype(F32); m=r.astype(BF16); l=(r-m.astype(F32)).astype(BF16)
    return h,m,l
def gj(L,R,p,sub,two):
    nv=p//8
    if not two:
        for j in range(p):
            u,r=j//8,j%8
            dinv=1.0/sb(L[u][j],r)
            isr=sub==r
            t=sb(R[u],r)*dinv
            for k in range(j+1,p):
                tk=sb(L[u][k],r)*dinv
                for a in range(nv):
                    y=L[a][k]-L[a][j]*tk
                    L[a][k]=jnp.where(isr,tk,y) if a==u else y
            R=[R[a]-L[a][j]*t for a in range(nv)]
            R[u]=jnp.where(isr,t,R[u])
        return R
    for j in range(0,p,2):
        u,r=j//8,j%8
        a_=sb(L[u][j],r); b_=sb(L[u][j+1],r); c_=sb(L[u][j+1],r+1)
        idet=1.0/(a_*c_-b_*b_)
        p00=c_*idet; p11=a_*idet; p01=b_*idet
        is0=sub==r; is1=sub==r+1
        def upd(cols):
            s0=sb(cols[u],r); s1=sb(cols[u],r+1)
            t0=p00*s0-p01*s1; t1=p11*s1-p01*s0
            out=[cols[a]-(L[a][j]*t0+L[a][j+1]*t1) for a in range(nv)]
            out[u]=jnp.where(is0,t0,jnp.where(is1,t1,out[u]))
            return out
        for k in range(j+2,p):
            o=upd([L[a][k] for a in range(nv)])
            for a in range(nv): L[a][k]=o[a]
        R=upd(R)
    return R
def inv128_ref(X_ref,two=False,p=16):
    lane=lax.broadcasted_iota(jnp.int32,(8,128),1)
    sub=lax.broadcasted_iota(jnp.int32,(8,128),0)
    lane_all=lax.broadcasted_iota(jnp.int32,(128,128),1)
    nv=p//8
    G=128//p
    R=[X_ref[8*a:8*a+8,:] for a in range(nv)]
    for g in range(G):
        base=g*p; n=(g+1)%G
        N=[X_ref[n*p+8*a:n*p+8*a+8,:] for a in range(nv)]
        ing=(lane>=base)&(lane<base+p)
        L=[[lb(R[a],base+j) for j in range(p)] for a in range(nv)]
        Rh=[jnp.where(ing,jnp.where(lane-base==sub+8*a,1.0,0.0),R[a]) for a in range(nv)]
        X=X_ref[...]
        h,m,l=split(X)
        LH=jnp.concatenate([h,h,m,h,l,m],axis=1)
        if g<G-1:
            CN=[[lb(N[a],base+j) for j in range(p)] for a in range(nv)]
        T=gj(L,Rh,p,sub,two)
        Tc=jnp.concatenate(T,axis=0)
        if g<G-1:
            Ts=[sb(T[j//8],j%8) for j in range(p)]
            Nn=[jnp.where(ing,0.0,N[a])-tsum([CN[a][j]*Ts[j] for j in range(p)]) for a in range(nv)]
        th,tm,tl=split(Tc)
        def pad(t):
            parts=[]
            if base: parts.append(jnp.zeros((base,128),BF16))
            parts.append(t)
            if base+p<128: parts.append(jnp.zeros((128-base-p,128),BF16))
            return jnp.concatenate(parts,axis=0)
        th,tm,tl=pad(th),pad(tm),pad(tl)
        RH=jnp.concatenate([th,tm,th,tl,th,tm],axis=0)
        U=jnp.dot(LH,RH,preferred_element_type=F32)
        inga=(lane_all>=base)&(lane_all<base+p)
        Xn=jnp.where(inga,0.0,X)-U
        X_ref[...]=Xn
        X_ref[base:base+p,:]=Tc
        if g<G-1:
            for a in range(nv): X_ref[n*p+8*a:n*p+8*a+8,:]=Nn[a]
            R=Nn


def lform(x):
    h,m,l=split(x); return jnp.concatenate([h,h,m,h,l,m],axis=1)
def rform(x):
    h,m,l=split(x); return jnp.concatenate([h,m,h,l,h,m],axis=1)
NT=(((1,),(1,)),((),()))
def nt(a,b): return lax.dot_general(a,b,NT,preferred_element_type=F32)
def factor_kernel(unroll,KA,KG,tokens,s_ref,g_ref,o_ref,A,X,G,Mh,Mm,Yh,Ym,MG):
    eye=jnp.where(lax.broadcasted_iota(jnp.int32,(B,B),0)==lax.broadcasted_iota(jnp.int32,(B,B),1),1.0,0.0).astype(F32)
    scale=1.0/tokens
    for j in range(8):
        for i in range(j,8):
            r=block_rows(i,j)
            v=s_ref[r:r+B,:]*scale
            A[r:r+B,:]=v+eye if i==j else v
    G[...]=g_ref[...].astype(F32)
    def body(j):
        R=(7-j)*B; d=block_rows(j,j); c=d+B
        dcat=rform(X[...])
        gl=lform(G[:,j*B:(j+1)*B])
        mg=nt(gl[:,:KG],dcat[:,:KG])
        MG[:,j*B:(j+1)*B]=mg
        if R:
            col=A[c:c+R,:]
            ccat=lform(col)
            m=nt(ccat[:,:KA],dcat[:,:KA])
            mcat=rform(m)
            Mh[c:c+R,:]=mcat[:,0:B]; Mm[c:c+R,:]=mcat[:,B:2*B]
            for k in range(j+1,8):
                o=(k-j-1)*B
                rk=block_rows(k,k); n=(8-k)*B
                A[rk:rk+n,:]-=nt(mcat[o:R,:KA],ccat[o:o+B,:KA])
            gm=rform(mg)
            G[:,(j+1)*B:]-=nt(gm[:,:KG],ccat[:,:KG])
    if unroll:
        for j in range(8):
            d=block_rows(j,j)
            X[...]=A[d:d+B,:]
            inv128_ref(X)
            body(j)
    else:
        def it(j,carry):
            d=pl.multiple_of((j*8-j*(j-1)//2)*B,B)
            X[...]=A[pl.ds(d,B),:]
            inv128_ref(X)
            for jj in range(8):
                @pl.when(j==jj)
                def _(): body(jj)
            return carry
        lax.fori_loop(0,8,it,0)
    for j in range(7,-1,-1):
        y=MG[:,j*B:(j+1)*B]
        if j<7:
            c=block_rows(j,j)+B; R=(7-j)*B
            yh,ym=Yh[:,(j+1)*B:],Ym[:,(j+1)*B:]
            mh,mm=Mh[c:c+R,:],Mm[c:c+R,:]
            y=y-(jnp.dot(yh,mh,preferred_element_type=F32)+jnp.dot(yh,mm,preferred_element_type=F32)+jnp.dot(ym,mh,preferred_element_type=F32))
        h=y.astype(BF16)
        Yh[:,j*B:(j+1)*B]=h
        Ym[:,j*B:(j+1)*B]=(y-h.astype(F32)).astype(BF16)
        o_ref[:,j*B:(j+1)*B]=h
def factor(s,g,tokens,unroll=False,KA=384,KG=384):
    vm=pl.BlockSpec(memory_space=pltpu.VMEM)
    n=g.shape[0]
    return pl.pallas_call(functools.partial(factor_kernel,unroll,KA,KG,tokens),
      out_shape=jax.ShapeDtypeStruct((n,1024),BF16),in_specs=[vm,vm],out_specs=vm,
      scratch_shapes=[pltpu.VMEM((4608,B),F32),pltpu.VMEM((B,B),F32),pltpu.VMEM((n,1024),F32),pltpu.VMEM((4608,B),BF16),pltpu.VMEM((4608,B),BF16),
        pltpu.VMEM((n,1024),BF16),pltpu.VMEM((n,1024),BF16),pltpu.VMEM((n,1024),F32)],
      compiler_params=pltpu.CompilerParams(vmem_limit_bytes=56<<20))(s,g)


def per_device(activations, gradient, block_map):
    tokens = activations.shape[0] * lax.axis_size("bcast")
    rows = gradient.shape[0]
    part = covariance(activations[:, 0, :])
    chooser = (block_map[None, :] == jnp.arange(16, dtype=jnp.int32)[:, None]).astype(BF16)
    ordered = jnp.einsum("kj,rjb->krb", chooser, gradient, preferred_element_type=F32).astype(BF16)
    total, tiles = exchange(part, ordered.reshape(16, rows * 8, 128))
    return factor(total, tiles.reshape(16 * rows, 1024), tokens)[:, None, :]


def solution(mesh):
    return jax.shard_map(
        per_device,
        mesh=mesh,
        in_specs=(P("bcast", "grad", None), P(("bcast", "grad"), None, None), P()),
        out_specs=P("bcast", "grad", None),
        check_vma=False,
    )
```

```python
import functools

import jax
import jax.numpy as jnp
from jax import lax
from jax.experimental import pallas as pl
from jax.experimental.pallas import tpu as pltpu
from jax.sharding import PartitionSpec as P

MESH = pl.DeviceIdType.MESH
F32, BF16 = jnp.float32, jnp.bfloat16
B = 128


def block_rows(i, j):
    return (j * 8 - j * (j - 1) // 2 + (i - j)) * B


def covariance_kernel(act_ref, out_ref):
    for j in range(8):
        column = act_ref[:, j * B : (j + 1) * B]
        part = lax.dot_general(
            act_ref[:, j * B :], column, (((0,), (0,)), ((), ())), preferred_element_type=F32
        )
        out_ref[pl.ds(block_rows(j, j), (8 - j) * B), :] = part


def exchange_body(part_ref, grad_ref, sum_ref, tile_ref, acc, from_core, from_x, za_plus, za_minus, zb_plus, zb_minus, xa,
                  s_sem, r_sem, own_sem):
    H = 1152
    CA, SA = 144, 72
    XB, CB = 576, 72
    me = lax.axis_index("bcast")
    column = lax.axis_index("grad")
    core, z, x = me % 2, (me // 2) % 8, me // 16

    def at(c, zz, xx):
        return {"bcast": xx * 16 + (zz % 8) * 2 + c}

    twin, up, down, across = at(1 - core, z, x), at(core, z + 1, x), at(core, z + 7, x), at(core, z, 1 - x)
    barrier = pltpu.get_barrier_semaphore()
    for peer in (twin, up, down, across):
        pl.semaphore_signal(barrier, inc=1, device_id=peer, device_id_type=MESH)
    for d in range(1, 16):
        pl.semaphore_signal(barrier, inc=1, device_id={"grad": (column + d) % 16}, device_id_type=MESH)
    pl.semaphore_wait(barrier, 19)

    sent = []

    def send(src, dst, to):
        n = len(sent)
        c = pltpu.make_async_remote_copy(src_ref=src, dst_ref=dst, send_sem=s_sem.at[n], recv_sem=r_sem.at[n],
                                         device_id=to, device_id_type=MESH)
        c.start()
        sent.append(c)
        return c

    def ds(start, n):
        return pl.ds(pl.multiple_of(start, 8), n)

    def a_rows(q, h=None):
        return ds((q % 8) * CA + (0 if h is None else h * SA), CA if h is None else SA)

    def b_rows(xx, q=None):
        return ds(H + xx * XB + (0 if q is None else (q % 8) * CB), XB if q is None else CB)

    def pa(c, q, h=None):
        return ds(c * H + (q % 8) * CA + (0 if h is None else h * SA), CA if h is None else SA)

    def pb(c, xx, q=None):
        return ds(2 * H + c * H + xx * XB + (0 if q is None else (q % 8) * CB), XB if q is None else CB)

    order = [4, 5, 3, 6, 2, 7, 1, 0]
    swap_a = {}

    def swap(d):
        swap_a[d] = send(part_ref.at[pa(1 - core, z + d)], from_core.at[a_rows(z + d)], twin)

    swap(4), swap(5)
    swap_b0 = send(part_ref.at[pb(1 - core, 1 - x)], from_core.at[b_rows(1 - x)], twin)
    for d in order[2:]:
        swap(d)
    swap_b1 = send(part_ref.at[pb(1 - core, x)], from_core.at[b_rows(x)], twin)

    def add_a(d):
        swap_a[d].wait_recv()
        acc[a_rows(z + d)] = part_ref[pa(core, z + d)] + from_core[a_rows(z + d)]

    def ring(buf, k, rows, to):
        return send(acc.at[rows], buf.at[k], to)

    add_a(4)
    ap = [send(acc.at[a_rows(z + 4, h)], za_plus.at[0, h], up) for h in (0, 1)]
    add_a(5)
    am = [send(acc.at[a_rows(z + 5, h)], za_minus.at[0, h], down) for h in (0, 1)]
    swap_b0.wait_recv()
    acc[b_rows(1 - x)] = part_ref[pb(core, 1 - x)] + from_core[b_rows(1 - x)]
    bx = {d: send(acc.at[b_rows(1 - x, z + d)], from_x.at[ds(((z + d) % 8) * CB, CB)], across) for d in order}
    own = pltpu.make_async_copy(grad_ref.at[column], tile_ref.at[column], own_sem)
    own.start()
    tiles = []
    for d in range(1, 16):
        to = (column + d) % 16
        tiles.append(send(grad_ref.at[to], tile_ref.at[column], {"grad": to}))
    for d in order[2:]:
        add_a(d)
    swap_b1.wait_recv()
    acc[b_rows(x)] = part_ref[pb(core, x)] + from_core[b_rows(x)]

    def step_a(s):
        nonlocal ap, am
        q = []
        for h in (0, 1):
            ap[h].wait_recv()
            acc[a_rows(z + 4 - s, h)] += za_plus[s - 1, h]
            if s < 4:
                q.append(send(acc.at[a_rows(z + 4 - s, h)], za_plus.at[s, h], up))
        ap = q
        if s < 4:
            q = []
            for h in (0, 1):
                am[h].wait_recv()
                acc[a_rows(z + 5 + s, h)] += za_minus[s - 1, h]
                if s < 3:
                    q.append(send(acc.at[a_rows(z + 5 + s, h)], za_minus.at[s, h], down))
            am = q

    def take_x(d):
        bx[d].wait_recv()
        acc[b_rows(x, z + d)] += from_x[ds(((z + d) % 8) * CB, CB)]

    bp = bm = None

    def step_b(s):
        nonlocal bp, bm
        if s < 4:
            take_x(4 - s)
        if s == 4:
            acc[b_rows(x, z)] += zb_plus_wait()
        else:
            if s:
                bp.wait_recv()
                acc[b_rows(x, z + 4 - s)] += zb_plus[s - 1]
            bp = send(acc.at[b_rows(x, z + 4 - s)], zb_plus.at[s], up)
        if s < 4:
            take_x((5 + s) % 8)
            if s:
                bm.wait_recv()
                acc[b_rows(x, z + 5 + s)] += zb_minus[s - 1]
            if s < 3:
                bm = send(acc.at[b_rows(x, z + 5 + s)], zb_minus.at[s], down)

    def zb_plus_wait():
        bp.wait_recv()
        return zb_plus[3]

    step_a(1)
    step_b(0)
    step_a(2)
    step_b(1)
    step_a(3)
    step_b(2)
    step_a(4)
    xa_c = send(acc.at[a_rows(z, 1 - x)], xa, across)
    step_b(3)
    xa_c.wait_recv()
    sum_ref[pa(core, z, x)] = acc[a_rows(z, x)] + xa[...]

    def same(rows, to):
        return send(sum_ref.at[rows], sum_ref.at[rows], to)

    xg = same(pa(core, z, x), across)
    step_b(4)
    sum_ref[pb(core, x, z)] = acc[b_rows(x, z)]
    twins, xs = [], []

    def b_out(q, plus, minus):
        r = pb(core, x, q)
        p = same(r, up) if plus else None
        m = same(r, down) if minus else None
        xs.append((same(r, across), q))
        twins.append(same(r, twin))
        return p, m

    bp, bm = b_out(z, True, True)
    xg.wait_recv()
    r = pa(core, z)
    ap, am = same(r, up), same(r, down)
    twins.append(same(r, twin))

    def relay():
        c, q = xs.pop(0)
        c.wait_recv()
        twins.append(same(pb(core, 1 - x, q), twin))

    for s in range(1, 5):
        bp.wait_recv()
        bp, _ = b_out(z + 8 - s, s < 4, False)
        if s < 4:
            bm.wait_recv()
            _, bm = b_out(z + s, False, s < 3)
        ap.wait_recv()
        r = pa(core, z + 8 - s)
        if s < 4:
            ap = same(r, up)
        twins.append(same(r, twin))
        if s < 4:
            am.wait_recv()
            r = pa(core, z + s)
            if s < 3:
                am = same(r, down)
            twins.append(same(r, twin))
        relay()
        if s > 1:
            relay()
    relay()
    for c in twins:
        c.wait_recv()
    for c in tiles:
        c.wait_recv()
    for c in sent:
        c.wait_send()
    own.wait()


N_COPIES = 160


def exchange(part, grads):
    dma = pltpu.SemaphoreType.DMA
    vm = pl.BlockSpec(memory_space=pltpu.VMEM)
    return pl.pallas_call(
        exchange_body,
        out_shape=(jax.ShapeDtypeStruct((4608, B), F32), jax.ShapeDtypeStruct(grads.shape, BF16)),
        in_specs=[vm, vm],
        out_specs=(vm, vm),
        scratch_shapes=[
            pltpu.VMEM((2304, B), F32), pltpu.VMEM((2304, B), F32), pltpu.VMEM((576, B), F32),
            pltpu.VMEM((4, 2, 72, B), F32), pltpu.VMEM((3, 2, 72, B), F32),
            pltpu.VMEM((4, 72, B), F32), pltpu.VMEM((3, 72, B), F32), pltpu.VMEM((72, B), F32),
            dma((N_COPIES,)), dma((N_COPIES,)), dma,
        ],
        compiler_params=pltpu.CompilerParams(collective_id=0, has_side_effects=True, vmem_limit_bytes=48 << 20),
    )(part, grads)


def covariance(act):
    vm = pl.BlockSpec(memory_space=pltpu.VMEM)
    return pl.pallas_call(
        covariance_kernel,
        out_shape=jax.ShapeDtypeStruct((4608, B), F32),
        in_specs=[vm], out_specs=vm,
        compiler_params=pltpu.CompilerParams(vmem_limit_bytes=48 << 20),
    )(act)


def lb(t,j): return jnp.broadcast_to(t[:,j:j+1],(8,128))
def sb(t,r): return jnp.broadcast_to(t[r:r+1,:],(8,128))
def tsum(xs):
    xs=list(xs)
    while len(xs)>1:
        xs=[xs[i]+xs[i+1] if i+1<len(xs) else xs[i] for i in range(0,len(xs),2)]
    return xs[0]
def split(x):
    h=x.astype(BF16); r=x-h.astype(F32); m=r.astype(BF16); l=(r-m.astype(F32)).astype(BF16)
    return h,m,l
def gj(L,R,p,sub,two):
    nv=p//8
    if not two:
        for j in range(p):
            u,r=j//8,j%8
            dinv=1.0/sb(L[u][j],r)
            isr=sub==r
            t=sb(R[u],r)*dinv
            for k in range(j+1,p):
                tk=sb(L[u][k],r)*dinv
                for a in range(nv):
                    y=L[a][k]-L[a][j]*tk
                    L[a][k]=jnp.where(isr,tk,y) if a==u else y
            R=[R[a]-L[a][j]*t for a in range(nv)]
            R[u]=jnp.where(isr,t,R[u])
        return R
    for j in range(0,p,2):
        u,r=j//8,j%8
        a_=sb(L[u][j],r); b_=sb(L[u][j+1],r); c_=sb(L[u][j+1],r+1)
        idet=1.0/(a_*c_-b_*b_)
        p00=c_*idet; p11=a_*idet; p01=b_*idet
        is0=sub==r; is1=sub==r+1
        def upd(cols):
            s0=sb(cols[u],r); s1=sb(cols[u],r+1)
            t0=p00*s0-p01*s1; t1=p11*s1-p01*s0
            out=[cols[a]-(L[a][j]*t0+L[a][j+1]*t1) for a in range(nv)]
            out[u]=jnp.where(is0,t0,jnp.where(is1,t1,out[u]))
            return out
        for k in range(j+2,p):
            o=upd([L[a][k] for a in range(nv)])
            for a in range(nv): L[a][k]=o[a]
        R=upd(R)
    return R
def inv128_ref(X_ref,two=False,p=16):
    lane=lax.broadcasted_iota(jnp.int32,(8,128),1)
    sub=lax.broadcasted_iota(jnp.int32,(8,128),0)
    lane_all=lax.broadcasted_iota(jnp.int32,(128,128),1)
    nv=p//8
    G=128//p
    R=[X_ref[8*a:8*a+8,:] for a in range(nv)]
    for g in range(G):
        base=g*p; n=(g+1)%G
        N=[X_ref[n*p+8*a:n*p+8*a+8,:] for a in range(nv)]
        ing=(lane>=base)&(lane<base+p)
        L=[[lb(R[a],base+j) for j in range(p)] for a in range(nv)]
        Rh=[jnp.where(ing,jnp.where(lane-base==sub+8*a,1.0,0.0),R[a]) for a in range(nv)]
        X=X_ref[...]
        h,m,l=split(X)
        LH=jnp.concatenate([h,h,m],axis=1)
        if g<G-1:
            CN=[[lb(N[a],base+j) for j in range(p)] for a in range(nv)]
        T=gj(L,Rh,p,sub,two)
        Tc=jnp.concatenate(T,axis=0)
        if g<G-1:
            Ts=[sb(T[j//8],j%8) for j in range(p)]
            Nn=[jnp.where(ing,0.0,N[a])-tsum([CN[a][j]*Ts[j] for j in range(p)]) for a in range(nv)]
        th,tm,tl=split(Tc)
        def pad(t):
            parts=[]
            if base: parts.append(jnp.zeros((base,128),BF16))
            parts.append(t)
            if base+p<128: parts.append(jnp.zeros((128-base-p,128),BF16))
            return jnp.concatenate(parts,axis=0)
        th,tm,tl=pad(th),pad(tm),pad(tl)
        RH=jnp.concatenate([th,tm,th],axis=0)
        U=jnp.dot(LH,RH,preferred_element_type=F32)
        inga=(lane_all>=base)&(lane_all<base+p)
        Xn=jnp.where(inga,0.0,X)-U
        X_ref[...]=Xn
        X_ref[base:base+p,:]=Tc
        if g<G-1:
            for a in range(nv): X_ref[n*p+8*a:n*p+8*a+8,:]=Nn[a]
            R=Nn


def lform(x):
    h,m,l=split(x); return jnp.concatenate([h,h,m,h,l,m],axis=1)
def rform(x):
    h,m,l=split(x); return jnp.concatenate([h,m,h,l,h,m],axis=1)
NT=(((1,),(1,)),((),()))
def nt(a,b): return lax.dot_general(a,b,NT,preferred_element_type=F32)
def factor_kernel(unroll,KA,KG,tokens,s_ref,g_ref,o_ref,A,X,G,Mh,Mm,Yh,Ym,MG):
    eye=jnp.where(lax.broadcasted_iota(jnp.int32,(B,B),0)==lax.broadcasted_iota(jnp.int32,(B,B),1),1.0,0.0).astype(F32)
    scale=1.0/tokens
    for j in range(8):
        for i in range(j,8):
            r=block_rows(i,j)
            v=s_ref[r:r+B,:]*scale
            A[r:r+B,:]=v+eye if i==j else v
    G[...]=g_ref[...].astype(F32)
    def body(j):
        R=(7-j)*B; d=block_rows(j,j); c=d+B
        dcat=rform(X[...])
        gl=lform(G[:,j*B:(j+1)*B])
        mg=nt(gl[:,:KG],dcat[:,:KG])
        MG[:,j*B:(j+1)*B]=mg
        if R:
            col=A[c:c+R,:]
            ccat=lform(col)
            m=nt(ccat[:,:KA],dcat[:,:KA])
            mcat=rform(m)
            Mh[c:c+R,:]=mcat[:,0:B]; Mm[c:c+R,:]=mcat[:,B:2*B]
            for k in range(j+1,8):
                o=(k-j-1)*B
                rk=block_rows(k,k); n=(8-k)*B
                A[rk:rk+n,:]-=nt(mcat[o:R,:KA],ccat[o:o+B,:KA])
            gm=rform(mg)
            G[:,(j+1)*B:]-=nt(gm[:,:KG],ccat[:,:KG])
    if unroll:
        for j in range(8):
            d=block_rows(j,j)
            X[...]=A[d:d+B,:]
            inv128_ref(X)
            body(j)
    else:
        def it(j,carry):
            d=pl.multiple_of((j*8-j*(j-1)//2)*B,B)
            X[...]=A[pl.ds(d,B),:]
            inv128_ref(X)
            for jj in range(8):
                @pl.when(j==jj)
                def _(): body(jj)
            return carry
        lax.fori_loop(0,8,it,0)
    for j in range(7,-1,-1):
        y=MG[:,j*B:(j+1)*B]
        if j<7:
            c=block_rows(j,j)+B; R=(7-j)*B
            yh,ym=Yh[:,(j+1)*B:],Ym[:,(j+1)*B:]
            mh,mm=Mh[c:c+R,:],Mm[c:c+R,:]
            y=y-(jnp.dot(yh,mh,preferred_element_type=F32)+jnp.dot(yh,mm,preferred_element_type=F32)+jnp.dot(ym,mh,preferred_element_type=F32))
        h=y.astype(BF16)
        Yh[:,j*B:(j+1)*B]=h
        Ym[:,j*B:(j+1)*B]=(y-h.astype(F32)).astype(BF16)
        o_ref[:,j*B:(j+1)*B]=h
def factor(s,g,tokens,unroll=False,KA=384,KG=384):
    vm=pl.BlockSpec(memory_space=pltpu.VMEM)
    n=g.shape[0]
    return pl.pallas_call(functools.partial(factor_kernel,unroll,KA,KG,tokens),
      out_shape=jax.ShapeDtypeStruct((n,1024),BF16),in_specs=[vm,vm],out_specs=vm,
      scratch_shapes=[pltpu.VMEM((4608,B),F32),pltpu.VMEM((B,B),F32),pltpu.VMEM((n,1024),F32),pltpu.VMEM((4608,B),BF16),pltpu.VMEM((4608,B),BF16),
        pltpu.VMEM((n,1024),BF16),pltpu.VMEM((n,1024),BF16),pltpu.VMEM((n,1024),F32)],
      compiler_params=pltpu.CompilerParams(vmem_limit_bytes=56<<20))(s,g)


def per_device(activations, gradient, block_map):
    tokens = activations.shape[0] * lax.axis_size("bcast")
    rows = gradient.shape[0]
    part = covariance(activations[:, 0, :])
    chooser = (block_map[None, :] == jnp.arange(16, dtype=jnp.int32)[:, None]).astype(BF16)
    ordered = jnp.einsum("kj,rjb->krb", chooser, gradient, preferred_element_type=F32).astype(BF16)
    total, tiles = exchange(part, ordered.reshape(16, rows * 8, 128))
    return factor(total, tiles.reshape(16 * rows, 1024), tokens)[:, None, :]


def solution(mesh):
    return jax.shard_map(
        per_device,
        mesh=mesh,
        in_specs=(P("bcast", "grad", None), P(("bcast", "grad"), None, None), P()),
        out_specs=P("bcast", "grad", None),
        check_vma=False,
    )
```

```python
import functools

import jax
import jax.numpy as jnp
from jax import lax
from jax.experimental import pallas as pl
from jax.experimental.pallas import tpu as pltpu
from jax.sharding import PartitionSpec as P

MESH = pl.DeviceIdType.MESH
F32, BF16 = jnp.float32, jnp.bfloat16
B = 128


def block_rows(i, j):
    return (j * 8 - j * (j - 1) // 2 + (i - j)) * B


def covariance_kernel(act_ref, out_ref):
    for j in range(8):
        column = act_ref[:, j * B : (j + 1) * B]
        part = lax.dot_general(
            act_ref[:, j * B :], column, (((0,), (0,)), ((), ())), preferred_element_type=F32
        )
        out_ref[pl.ds(block_rows(j, j), (8 - j) * B), :] = part


def covariance(act):
    vm = pl.BlockSpec(memory_space=pltpu.VMEM)
    return pl.pallas_call(
        covariance_kernel,
        out_shape=jax.ShapeDtypeStruct((4608, B), F32),
        in_specs=[vm], out_specs=vm,
        compiler_params=pltpu.CompilerParams(vmem_limit_bytes=48 << 20),
    )(act)


def lb(t,j): return jnp.broadcast_to(t[:,j:j+1],(8,128))
def sb(t,r): return jnp.broadcast_to(t[r:r+1,:],(8,128))
def tsum(xs):
    xs=list(xs)
    while len(xs)>1:
        xs=[xs[i]+xs[i+1] if i+1<len(xs) else xs[i] for i in range(0,len(xs),2)]
    return xs[0]
def split(x):
    h=x.astype(BF16); r=x-h.astype(F32); m=r.astype(BF16); l=(r-m.astype(F32)).astype(BF16)
    return h,m,l
def gj(L,R,p,sub,two):
    nv=p//8
    if not two:
        for j in range(p):
            u,r=j//8,j%8
            dinv=1.0/sb(L[u][j],r)
            isr=sub==r
            t=sb(R[u],r)*dinv
            for k in range(j+1,p):
                tk=sb(L[u][k],r)*dinv
                for a in range(nv):
                    y=L[a][k]-L[a][j]*tk
                    L[a][k]=jnp.where(isr,tk,y) if a==u else y
            R=[R[a]-L[a][j]*t for a in range(nv)]
            R[u]=jnp.where(isr,t,R[u])
        return R
    for j in range(0,p,2):
        u,r=j//8,j%8
        a_=sb(L[u][j],r); b_=sb(L[u][j+1],r); c_=sb(L[u][j+1],r+1)
        idet=1.0/(a_*c_-b_*b_)
        p00=c_*idet; p11=a_*idet; p01=b_*idet
        is0=sub==r; is1=sub==r+1
        def upd(cols):
            s0=sb(cols[u],r); s1=sb(cols[u],r+1)
            t0=p00*s0-p01*s1; t1=p11*s1-p01*s0
            out=[cols[a]-(L[a][j]*t0+L[a][j+1]*t1) for a in range(nv)]
            out[u]=jnp.where(is0,t0,jnp.where(is1,t1,out[u]))
            return out
        for k in range(j+2,p):
            o=upd([L[a][k] for a in range(nv)])
            for a in range(nv): L[a][k]=o[a]
        R=upd(R)
    return R
def inv128_ref(X_ref,hook=None,two=False,p=16):
    lane=lax.broadcasted_iota(jnp.int32,(8,128),1)
    sub=lax.broadcasted_iota(jnp.int32,(8,128),0)
    lane_all=lax.broadcasted_iota(jnp.int32,(128,128),1)
    nv=p//8
    G=128//p
    R=[X_ref[8*a:8*a+8,:] for a in range(nv)]
    for g in range(G):
        base=g*p; n=(g+1)%G
        N=[X_ref[n*p+8*a:n*p+8*a+8,:] for a in range(nv)]
        ing=(lane>=base)&(lane<base+p)
        L=[[lb(R[a],base+j) for j in range(p)] for a in range(nv)]
        Rh=[jnp.where(ing,jnp.where(lane-base==sub+8*a,1.0,0.0),R[a]) for a in range(nv)]
        X=X_ref[...]
        h,m,l=split(X)
        LH=jnp.concatenate([h,h,m],axis=1)
        if g<G-1:
            CN=[[lb(N[a],base+j) for j in range(p)] for a in range(nv)]
        T=gj(L,Rh,p,sub,two)
        Tc=jnp.concatenate(T,axis=0)
        if g<G-1:
            Ts=[sb(T[j//8],j%8) for j in range(p)]
            Nn=[jnp.where(ing,0.0,N[a])-tsum([CN[a][j]*Ts[j] for j in range(p)]) for a in range(nv)]
        th,tm,tl=split(Tc)
        def pad(t):
            parts=[]
            if base: parts.append(jnp.zeros((base,128),BF16))
            parts.append(t)
            if base+p<128: parts.append(jnp.zeros((128-base-p,128),BF16))
            return jnp.concatenate(parts,axis=0)
        th,tm,tl=pad(th),pad(tm),pad(tl)
        RH=jnp.concatenate([th,tm,th],axis=0)
        U=jnp.dot(LH,RH,preferred_element_type=F32)
        inga=(lane_all>=base)&(lane_all<base+p)
        Xn=jnp.where(inga,0.0,X)-U
        X_ref[...]=Xn
        X_ref[base:base+p,:]=Tc
        if g<G-1:
            for a in range(nv): X_ref[n*p+8*a:n*p+8*a+8,:]=Nn[a]
            R=Nn
        if hook is not None: hook(g)


def lform(x):
    h,m,l=split(x); return jnp.concatenate([h,h,m,h,l,m],axis=1)
def rform(x):
    h,m,l=split(x); return jnp.concatenate([h,m,h,l,h,m],axis=1)
NT=(((1,),(1,)),((),()))
def nt(a,b): return lax.dot_general(a,b,NT,preferred_element_type=F32)

TOTAL = 4608
FIRST = 1024
H = 896
CA, SA = 112, 56
XB, CB = 448, 56
FH, FC = 512, 32


def step_kernel(tokens, part_ref, grad_ref, out_ref, S, tile, acc, from_core, from_x, za_plus, za_minus, zb_plus, zb_minus, xa,
                acc0, core0, slots0, A, X, G, Mh, Mm, Yh, Ym, MG, s_sem, r_sem, own_sem):
    me = lax.axis_index("bcast")
    column = lax.axis_index("grad")
    core, z, x = me % 2, (me // 2) % 8, me // 16

    def at(c, zz, xx):
        return {"bcast": (xx % 2) * 16 + (zz % 8) * 2 + c}

    twin, up, down, across = at(1 - core, z, x), at(core, z + 1, x), at(core, z + 7, x), at(core, z, x + 1)
    others = [(dz, dx) for dz in (4, 3, 5, 2, 6, 1, 7, 0) for dx in (1, 0) if (dz, dx) != (0, 0)]
    barrier = pltpu.get_barrier_semaphore()
    pl.semaphore_signal(barrier, inc=1, device_id=twin, device_id_type=MESH)
    for dz, dx in others:
        pl.semaphore_signal(barrier, inc=1, device_id=at(core, z + dz, x + dx), device_id_type=MESH)
    for d in range(1, 16):
        pl.semaphore_signal(barrier, inc=1, device_id={"grad": (column + d) % 16}, device_id_type=MESH)
    pl.semaphore_wait(barrier, 31)

    sent = []

    def send(src, dst, to):
        n = len(sent)
        c = pltpu.make_async_remote_copy(src_ref=src, dst_ref=dst, send_sem=s_sem.at[n], recv_sem=r_sem.at[n],
                                         device_id=to, device_id_type=MESH)
        c.start()
        sent.append(c)
        return c

    def ds(start, n):
        return pl.ds(pl.multiple_of(start, 8), n)

    def a_rows(q, h=None):
        return ds((q % 8) * CA + (0 if h is None else h * SA), CA if h is None else SA)

    def b_rows(xx, q=None):
        return ds(H + xx * XB + (0 if q is None else (q % 8) * CB), XB if q is None else CB)

    def pa(c, q, h=None):
        return ds(FIRST + c * H + (q % 8) * CA + (0 if h is None else h * SA), CA if h is None else SA)

    def pb(c, xx, q=None):
        return ds(FIRST + 2 * H + c * H + xx * XB + (0 if q is None else (q % 8) * CB), XB if q is None else CB)

    def mine0(zz, xx):
        return ds(((zz % 8) * 2 + xx % 2) * FC, FC)

    def p0(c, zz, xx):
        return ds(c * FH + ((zz % 8) * 2 + xx % 2) * FC, FC)

    def half0(c):
        return ds(c * FH, FH)

    order = [4, 5, 3, 6, 2, 7, 1, 0]
    swap_0 = send(part_ref.at[half0(1 - core)], core0, twin)
    swap_a = {}

    def swap(d):
        swap_a[d] = send(part_ref.at[pa(1 - core, z + d)], from_core.at[a_rows(z + d)], twin)

    swap(4), swap(5)
    swap_b0 = send(part_ref.at[pb(1 - core, 1 - x)], from_core.at[b_rows(1 - x)], twin)
    for d in order[2:]:
        swap(d)
    swap_b1 = send(part_ref.at[pb(1 - core, x)], from_core.at[b_rows(x)], twin)

    swap_0.wait_recv()
    acc0[...] = part_ref[half0(core)] + core0[...]
    first = [send(acc0.at[mine0(z + dz, x + dx)], slots0.at[dz * 2 + dx], at(core, z + dz, x + dx)) for dz, dx in others]

    def add_a(d):
        swap_a[d].wait_recv()
        acc[a_rows(z + d)] = part_ref[pa(core, z + d)] + from_core[a_rows(z + d)]

    add_a(4)
    ap = [send(acc.at[a_rows(z + 4, h)], za_plus.at[0, h], up) for h in (0, 1)]
    add_a(5)
    am = [send(acc.at[a_rows(z + 5, h)], za_minus.at[0, h], down) for h in (0, 1)]
    swap_b0.wait_recv()
    acc[b_rows(1 - x)] = part_ref[pb(core, 1 - x)] + from_core[b_rows(1 - x)]
    bx = {d: send(acc.at[b_rows(1 - x, z + d)], from_x.at[ds(((z + d) % 8) * CB, CB)], across) for d in order}
    own = pltpu.make_async_copy(grad_ref.at[column], tile.at[column], own_sem)
    own.start()
    tiles = []
    for d in range(1, 16):
        to = (column + d) % 16
        tiles.append(send(grad_ref.at[to], tile.at[column], {"grad": to}))
    for d in order[2:]:
        add_a(d)
    swap_b1.wait_recv()
    acc[b_rows(x)] = part_ref[pb(core, x)] + from_core[b_rows(x)]

    def step_a(s):
        nonlocal ap, am
        q = []
        for h in (0, 1):
            ap[h].wait_recv()
            acc[a_rows(z + 4 - s, h)] += za_plus[s - 1, h]
            if s < 4:
                q.append(send(acc.at[a_rows(z + 4 - s, h)], za_plus.at[s, h], up))
        ap = q
        if s < 4:
            q = []
            for h in (0, 1):
                am[h].wait_recv()
                acc[a_rows(z + 5 + s, h)] += za_minus[s - 1, h]
                if s < 3:
                    q.append(send(acc.at[a_rows(z + 5 + s, h)], za_minus.at[s, h], down))
            am = q

    def take_x(d):
        bx[d].wait_recv()
        acc[b_rows(x, z + d)] += from_x[ds(((z + d) % 8) * CB, CB)]

    bp = bm = None

    def step_b(s):
        nonlocal bp, bm
        if s < 4:
            take_x(4 - s)
        if s:
            bp.wait_recv()
            acc[b_rows(x, z + 4 - s)] += zb_plus[s - 1]
        if s < 4:
            bp = send(acc.at[b_rows(x, z + 4 - s)], zb_plus.at[s], up)
            take_x((5 + s) % 8)
            if s:
                bm.wait_recv()
                acc[b_rows(x, z + 5 + s)] += zb_minus[s - 1]
            if s < 3:
                bm = send(acc.at[b_rows(x, z + 5 + s)], zb_minus.at[s], down)

    def same(rows, to):
        return send(S.at[rows], S.at[rows], to)

    step_a(1)
    step_b(0)
    total = acc0[mine0(z, x)]
    for c, (dz, dx) in zip(first, others):
        c.wait_recv()
        total = total + slots0[dz * 2 + dx]
    S[p0(core, z, x)] = total
    gather0 = [same(p0(core, z, x), at(core, z + dz, x + dx)) for dz, dx in others]
    step_a(2)
    step_b(1)
    step_a(3)
    step_b(2)
    for c in gather0:
        c.wait_recv()
    twin0 = same(half0(core), twin)
    step_a(4)
    xa_c = send(acc.at[a_rows(z, 1 - x)], xa, across)

    def rest():
        nonlocal ap, am, bp, bm
        twins_a, twins_b, xs = [], [], []

        def b_out(q, plus, minus):
            r = pb(core, x, q)
            p = same(r, up) if plus else None
            m = same(r, down) if minus else None
            xs.append((same(r, across), q))
            twins_b.append(same(r, twin))
            return p, m

        def relay():
            c, q = xs.pop(0)
            c.wait_recv()
            twins_b.append(same(pb(core, 1 - x, q), twin))

        step_b(3)
        yield False
        xa_c.wait_recv()
        S[pa(core, z, x)] = acc[a_rows(z, x)] + xa[...]
        xg = same(pa(core, z, x), across)
        yield False
        step_b(4)
        S[pb(core, x, z)] = acc[b_rows(x, z)]
        bp, bm = b_out(z, True, True)
        yield False
        xg.wait_recv()
        r = pa(core, z)
        ap, am = same(r, up), same(r, down)
        twins_a.append(same(r, twin))
        yield False
        for s in range(1, 5):
            bp.wait_recv()
            bp, _ = b_out(z + 8 - s, s < 4, False)
            if s < 4:
                bm.wait_recv()
                _, bm = b_out(z + s, False, s < 3)
            yield False
            ap.wait_recv()
            r = pa(core, z + 8 - s)
            if s < 4:
                ap = same(r, up)
            twins_a.append(same(r, twin))
            if s < 4:
                am.wait_recv()
                r = pa(core, z + s)
                if s < 3:
                    am = same(r, down)
                twins_a.append(same(r, twin))
            yield False
        for c in twins_a:
            c.wait_recv()
        yield True
        while xs:
            relay()
            if xs:
                relay()
            yield True
        for c in twins_b:
            c.wait_recv()
        yield True

    work = rest()

    def advance():
        return next(work, True)

    scale = 1.0 / tokens
    eye = jnp.where(lax.broadcasted_iota(jnp.int32, (B, B), 0) == lax.broadcasted_iota(jnp.int32, (B, B), 1), 1.0, 0.0).astype(F32)
    K = 3 * B

    def take(j):
        d, n = block_rows(j, j), (8 - j) * B
        diagonal, below = S[d : d + B, :] * scale + eye, S[d + B : d + n, :] * scale if n > B else None
        if j:
            diagonal = diagonal + A[d : d + B, :]
            below = below + A[d + B : d + n, :] if n > B else None
        X[...] = diagonal
        if n > B:
            A[d + B : d + n, :] = below

    def body(j):
        R, c = (7 - j) * B, block_rows(j, j) + B
        dcat = rform(X[...])
        mg = nt(lform(G[:, j * B : (j + 1) * B])[:, :K], dcat[:, :K])
        MG[:, j * B : (j + 1) * B] = mg
        if R:
            ccat = lform(A[c : c + R, :])[:, :K]
            mcat = rform(nt(ccat, dcat[:, :K]))[:, :K]
            Mh[c : c + R, :] = mcat[:, 0:B]
            Mm[c : c + R, :] = mcat[:, B : 2 * B]
            for k in range(j + 1, 8):
                o, rk, n = (k - j - 1) * B, block_rows(k, k), (8 - k) * B
                u = nt(mcat[o:R], ccat[o : o + B])
                A[rk : rk + n, :] = A[rk : rk + n, :] - u if j else -u
            G[:, (j + 1) * B :] -= nt(rform(mg)[:, :K], ccat)

    twin0.wait_recv()
    take(0)

    def hook0(g):
        if g in (1, 5, 6):
            advance()

    inv128_ref(X, hook0)
    for c in tiles:
        c.wait_recv()
    own.wait()
    rows = out_ref.shape[0] // 16
    for n in range(16):
        G[n * rows : (n + 1) * rows, :] = tile[n].astype(F32)[:rows, :]
    advance()
    body(0)
    while not advance():
        pass
    take(1)

    def hook1(g):
        advance()

    inv128_ref(X, hook1)
    body(1)
    for _ in range(12):
        advance()
    for c in sent:
        c.wait_send()
    take(2)

    def later(j, carry):
        inv128_ref(X)
        for jj in range(2, 8):

            @pl.when(j == jj)
            def _():
                body(jj)
                if jj < 7:
                    take(jj + 1)

        return carry

    lax.fori_loop(2, 8, later, 0)
    for j in range(7, -1, -1):
        y = MG[:, j * B : (j + 1) * B]
        if j < 7:
            c, R = block_rows(j, j) + B, (7 - j) * B
            yh, ym = Yh[:, (j + 1) * B :], Ym[:, (j + 1) * B :]
            mh, mm = Mh[c : c + R, :], Mm[c : c + R, :]
            y = y - (jnp.dot(yh, mh, preferred_element_type=F32) + jnp.dot(yh, mm, preferred_element_type=F32)
                     + jnp.dot(ym, mh, preferred_element_type=F32))
        h = y.astype(BF16)
        Yh[:, j * B : (j + 1) * B] = h
        Ym[:, j * B : (j + 1) * B] = (y - h.astype(F32)).astype(BF16)
        out_ref[:, j * B : (j + 1) * B] = h


N_COPIES = 176


def step(part, grads, rows, tokens):
    dma = pltpu.SemaphoreType.DMA
    vm = pl.BlockSpec(memory_space=pltpu.VMEM)
    n = 16 * rows
    return pl.pallas_call(
        functools.partial(step_kernel, tokens),
        out_shape=jax.ShapeDtypeStruct((n, 1024), BF16),
        in_specs=[vm, vm],
        out_specs=vm,
        scratch_shapes=[
            pltpu.VMEM((TOTAL, B), F32), pltpu.VMEM(grads.shape, BF16),
            pltpu.VMEM((2 * H, B), F32), pltpu.VMEM((2 * H, B), F32), pltpu.VMEM((XB, B), F32),
            pltpu.VMEM((4, 2, SA, B), F32), pltpu.VMEM((3, 2, SA, B), F32),
            pltpu.VMEM((4, CB, B), F32), pltpu.VMEM((3, CB, B), F32), pltpu.VMEM((SA, B), F32),
            pltpu.VMEM((FH, B), F32), pltpu.VMEM((FH, B), F32), pltpu.VMEM((16, FC, B), F32),
            pltpu.VMEM((TOTAL, B), F32), pltpu.VMEM((B, B), F32), pltpu.VMEM((n, 1024), F32),
            pltpu.VMEM((TOTAL, B), BF16), pltpu.VMEM((TOTAL, B), BF16),
            pltpu.VMEM((n, 1024), BF16), pltpu.VMEM((n, 1024), BF16), pltpu.VMEM((n, 1024), F32),
            dma((N_COPIES,)), dma((N_COPIES,)), dma,
        ],
        compiler_params=pltpu.CompilerParams(collective_id=0, has_side_effects=True, vmem_limit_bytes=56 << 20),
    )(part, grads)


def per_device(activations, gradient, block_map):
    tokens = activations.shape[0] * lax.axis_size("bcast")
    rows = gradient.shape[0]
    part = covariance(activations[:, 0, :])
    chooser = (block_map[None, :] == jnp.arange(16, dtype=jnp.int32)[:, None]).astype(BF16)
    ordered = jnp.einsum("kj,rjb->krb", chooser, gradient, preferred_element_type=F32).astype(BF16)
    ordered = jnp.pad(ordered, ((0, 0), (0, -rows % 16), (0, 0)))
    return step(part, ordered, rows, tokens)[:, None, :]


def solution(mesh):
    return jax.shard_map(
        per_device,
        mesh=mesh,
        in_specs=(P("bcast", "grad", None), P(("bcast", "grad"), None, None), P()),
        out_specs=P("bcast", "grad", None),
        check_vma=False,
    )
```

```python
import functools

import jax
import jax.numpy as jnp
from jax import lax
from jax.experimental import pallas as pl
from jax.experimental.pallas import tpu as pltpu
from jax.sharding import PartitionSpec as P

MESH = pl.DeviceIdType.MESH
F32, BF16 = jnp.float32, jnp.bfloat16
B = 128


def block_rows(i, j):
    return (j * 8 - j * (j - 1) // 2 + (i - j)) * B


def covariance_kernel(act_ref, out_ref):
    for j in range(8):
        column = act_ref[:, j * B : (j + 1) * B]
        part = lax.dot_general(
            act_ref[:, j * B :], column, (((0,), (0,)), ((), ())), preferred_element_type=F32
        )
        out_ref[pl.ds(block_rows(j, j), (8 - j) * B), :] = part


def exchange_body(part_ref, grad_ref, sum_ref, tile_ref, acc, from_core, from_x, za_plus, za_minus, zb_plus, zb_minus, xa,
                  s_sem, r_sem, own_sem):
    H = 1152
    CA, SA = 144, 72
    XB, CB = 576, 72
    me = lax.axis_index("bcast")
    column = lax.axis_index("grad")
    core, z, x = me % 2, (me // 2) % 8, me // 16

    def at(c, zz, xx):
        return {"bcast": xx * 16 + (zz % 8) * 2 + c}

    twin, up, down, across = at(1 - core, z, x), at(core, z + 1, x), at(core, z + 7, x), at(core, z, 1 - x)
    barrier = pltpu.get_barrier_semaphore()
    for peer in (twin, up, down, across):
        pl.semaphore_signal(barrier, inc=1, device_id=peer, device_id_type=MESH)
    for d in range(1, 16):
        pl.semaphore_signal(barrier, inc=1, device_id={"grad": (column + d) % 16}, device_id_type=MESH)
    pl.semaphore_wait(barrier, 19)

    sent = []

    def send(src, dst, to):
        n = len(sent)
        c = pltpu.make_async_remote_copy(src_ref=src, dst_ref=dst, send_sem=s_sem.at[n], recv_sem=r_sem.at[n],
                                         device_id=to, device_id_type=MESH)
        c.start()
        sent.append(c)
        return c

    def ds(start, n):
        return pl.ds(pl.multiple_of(start, 8), n)

    def a_rows(q, h=None):
        return ds((q % 8) * CA + (0 if h is None else h * SA), CA if h is None else SA)

    def b_rows(xx, q=None):
        return ds(H + xx * XB + (0 if q is None else (q % 8) * CB), XB if q is None else CB)

    def pa(c, q, h=None):
        return ds(c * H + (q % 8) * CA + (0 if h is None else h * SA), CA if h is None else SA)

    def pb(c, xx, q=None):
        return ds(2 * H + c * H + xx * XB + (0 if q is None else (q % 8) * CB), XB if q is None else CB)

    order = [4, 5, 3, 6, 2, 7, 1, 0]
    swap_a = {}

    def swap(d):
        swap_a[d] = send(part_ref.at[pa(1 - core, z + d)], from_core.at[a_rows(z + d)], twin)

    swap(4), swap(5)
    swap_b0 = send(part_ref.at[pb(1 - core, 1 - x)], from_core.at[b_rows(1 - x)], twin)
    for d in order[2:]:
        swap(d)
    swap_b1 = send(part_ref.at[pb(1 - core, x)], from_core.at[b_rows(x)], twin)

    def add_a(d):
        swap_a[d].wait_recv()
        acc[a_rows(z + d)] = part_ref[pa(core, z + d)] + from_core[a_rows(z + d)]

    def ring(buf, k, rows, to):
        return send(acc.at[rows], buf.at[k], to)

    add_a(4)
    ap = [send(acc.at[a_rows(z + 4, h)], za_plus.at[0, h], up) for h in (0, 1)]
    add_a(5)
    am = [send(acc.at[a_rows(z + 5, h)], za_minus.at[0, h], down) for h in (0, 1)]
    swap_b0.wait_recv()
    acc[b_rows(1 - x)] = part_ref[pb(core, 1 - x)] + from_core[b_rows(1 - x)]
    bx = {d: send(acc.at[b_rows(1 - x, z + d)], from_x.at[ds(((z + d) % 8) * CB, CB)], across) for d in order}
    for d in order[2:]:
        add_a(d)
    swap_b1.wait_recv()
    acc[b_rows(x)] = part_ref[pb(core, x)] + from_core[b_rows(x)]

    def step_a(s):
        nonlocal ap, am
        q = []
        for h in (0, 1):
            ap[h].wait_recv()
            acc[a_rows(z + 4 - s, h)] += za_plus[s - 1, h]
            if s < 4:
                q.append(send(acc.at[a_rows(z + 4 - s, h)], za_plus.at[s, h], up))
        ap = q
        if s < 4:
            q = []
            for h in (0, 1):
                am[h].wait_recv()
                acc[a_rows(z + 5 + s, h)] += za_minus[s - 1, h]
                if s < 3:
                    q.append(send(acc.at[a_rows(z + 5 + s, h)], za_minus.at[s, h], down))
            am = q

    def take_x(d):
        bx[d].wait_recv()
        acc[b_rows(x, z + d)] += from_x[ds(((z + d) % 8) * CB, CB)]

    bp = bm = None

    def step_b(s):
        nonlocal bp, bm
        if s < 4:
            take_x(4 - s)
        if s == 4:
            acc[b_rows(x, z)] += zb_plus_wait()
        else:
            if s:
                bp.wait_recv()
                acc[b_rows(x, z + 4 - s)] += zb_plus[s - 1]
            bp = send(acc.at[b_rows(x, z + 4 - s)], zb_plus.at[s], up)
        if s < 4:
            take_x((5 + s) % 8)
            if s:
                bm.wait_recv()
                acc[b_rows(x, z + 5 + s)] += zb_minus[s - 1]
            if s < 3:
                bm = send(acc.at[b_rows(x, z + 5 + s)], zb_minus.at[s], down)

    def zb_plus_wait():
        bp.wait_recv()
        return zb_plus[3]

    step_a(1)
    step_b(0)
    step_a(2)
    step_b(1)
    step_a(3)
    step_b(2)
    own = pltpu.make_async_copy(grad_ref.at[column], tile_ref.at[column], own_sem)
    own.start()
    tiles = []
    for d in range(1, 16):
        to = (column + d) % 16
        tiles.append(send(grad_ref.at[to], tile_ref.at[column], {"grad": to}))
    step_a(4)
    xa_c = send(acc.at[a_rows(z, 1 - x)], xa, across)
    step_b(3)
    xa_c.wait_recv()
    sum_ref[pa(core, z, x)] = acc[a_rows(z, x)] + xa[...]

    def same(rows, to):
        return send(sum_ref.at[rows], sum_ref.at[rows], to)

    xg = same(pa(core, z, x), across)
    step_b(4)
    sum_ref[pb(core, x, z)] = acc[b_rows(x, z)]
    twins, xs = [], []

    def b_out(q, plus, minus):
        r = pb(core, x, q)
        p = same(r, up) if plus else None
        m = same(r, down) if minus else None
        xs.append((same(r, across), q))
        twins.append(same(r, twin))
        return p, m

    bp, bm = b_out(z, True, True)
    xg.wait_recv()
    r = pa(core, z)
    ap, am = same(r, up), same(r, down)
    twins.append(same(r, twin))

    def relay():
        c, q = xs.pop(0)
        c.wait_recv()
        twins.append(same(pb(core, 1 - x, q), twin))

    for s in range(1, 5):
        bp.wait_recv()
        bp, _ = b_out(z + 8 - s, s < 4, False)
        if s < 4:
            bm.wait_recv()
            _, bm = b_out(z + s, False, s < 3)
        ap.wait_recv()
        r = pa(core, z + 8 - s)
        if s < 4:
            ap = same(r, up)
        twins.append(same(r, twin))
        if s < 4:
            am.wait_recv()
            r = pa(core, z + s)
            if s < 3:
                am = same(r, down)
            twins.append(same(r, twin))
        relay()
        if s > 1:
            relay()
    relay()
    for c in twins:
        c.wait_recv()
    for c in tiles:
        c.wait_recv()
    for c in sent:
        c.wait_send()
    own.wait()


N_COPIES = 160


def exchange(part, grads):
    dma = pltpu.SemaphoreType.DMA
    vm = pl.BlockSpec(memory_space=pltpu.VMEM)
    return pl.pallas_call(
        exchange_body,
        out_shape=(jax.ShapeDtypeStruct((4608, B), F32), jax.ShapeDtypeStruct(grads.shape, BF16)),
        in_specs=[vm, vm],
        out_specs=(vm, vm),
        scratch_shapes=[
            pltpu.VMEM((2304, B), F32), pltpu.VMEM((2304, B), F32), pltpu.VMEM((576, B), F32),
            pltpu.VMEM((4, 2, 72, B), F32), pltpu.VMEM((3, 2, 72, B), F32),
            pltpu.VMEM((4, 72, B), F32), pltpu.VMEM((3, 72, B), F32), pltpu.VMEM((72, B), F32),
            dma((N_COPIES,)), dma((N_COPIES,)), dma,
        ],
        compiler_params=pltpu.CompilerParams(collective_id=0, has_side_effects=True, vmem_limit_bytes=18 << 20),
    )(part, grads)


def covariance(act):
    vm = pl.BlockSpec(memory_space=pltpu.VMEM)
    return pl.pallas_call(
        covariance_kernel,
        out_shape=jax.ShapeDtypeStruct((4608, B), F32),
        in_specs=[vm], out_specs=vm,
        compiler_params=pltpu.CompilerParams(vmem_limit_bytes=20 << 20),
    )(act)


def lb(t, j):
    return jnp.broadcast_to(t[:, j : j + 1], (8, B))


def sb(t, r):
    return jnp.broadcast_to(t[r : r + 1, :], (8, B))


def tsum(xs):
    xs = list(xs)
    while len(xs) > 1:
        xs = [xs[i] + xs[i + 1] if i + 1 < len(xs) else xs[i] for i in range(0, len(xs), 2)]
    return xs[0]

NT=(((1,),(1,)),((),()))
def nt(a,b): return lax.dot_general(a,b,NT,preferred_element_type=F32)
def split2(x):
    h=x.astype(BF16); return h,(x-h.astype(F32)).astype(BF16)
def lform3(x):
    h,m=split2(x); return jnp.concatenate([h,h,m],axis=1)
def rform3(x):
    h,m=split2(x); return jnp.concatenate([h,m,h],axis=1)
def gj(L, R, sub):
    for j in range(16):
        u, r = j // 8, j % 8
        dinv = 1.0 / sb(L[u][j], r)
        isr = sub == r
        t = sb(R[u], r) * dinv
        for k in range(j + 1, 16):
            tk = sb(L[u][k], r) * dinv
            for a in range(2):
                y = L[a][k] - L[a][j] * tk
                L[a][k] = jnp.where(isr, tk, y) if a == u else y
        R = [R[a] - L[a][j] * t for a in range(2)]
        R[u] = jnp.where(isr, t, R[u])
    return R


def inv128_h(X_ref,hook=None,p=16):
    lane=lax.broadcasted_iota(jnp.int32,(8,128),1)
    sub=lax.broadcasted_iota(jnp.int32,(8,128),0)
    lane_all=lax.broadcasted_iota(jnp.int32,(128,128),1)
    nv=p//8; Gn=128//p
    R=[X_ref[8*a:8*a+8,:] for a in range(nv)]
    for g in range(Gn):
        base=g*p; n=(g+1)%Gn
        N=[X_ref[n*p+8*a:n*p+8*a+8,:] for a in range(nv)]
        ing=(lane>=base)&(lane<base+p)
        L=[[lb(R[a],base+j) for j in range(p)] for a in range(nv)]
        Rh=[jnp.where(ing,jnp.where(lane-base==sub+8*a,1.0,0.0),R[a]) for a in range(nv)]
        X=X_ref[...]
        h,m=split2(X)
        LH=jnp.concatenate([h,h,m],axis=1)
        if g<Gn-1: CN=[[lb(N[a],base+j) for j in range(p)] for a in range(nv)]
        if hook is not None: hook(g)
        T=gj(L,Rh,sub)
        Tc=jnp.concatenate(T,axis=0)
        if g<Gn-1:
            Ts=[sb(T[j//8],j%8) for j in range(p)]
            Nn=[jnp.where(ing,0.0,N[a])-tsum([CN[a][j]*Ts[j] for j in range(p)]) for a in range(nv)]
        th,tm=split2(Tc)
        def pad(t):
            parts=[]
            if base: parts.append(jnp.zeros((base,128),BF16))
            parts.append(t)
            if base+p<128: parts.append(jnp.zeros((128-base-p,128),BF16))
            return jnp.concatenate(parts,axis=0)
        th,tm=pad(th),pad(tm)
        U=jnp.dot(LH,jnp.concatenate([th,tm,th],axis=0),preferred_element_type=F32)
        inga=(lane_all>=base)&(lane_all<base+p)
        X_ref[...]=jnp.where(inga,0.0,X)-U
        X_ref[base:base+p,:]=Tc
        if g<Gn-1:
            for a in range(nv): X_ref[n*p+8*a:n*p+8*a+8,:]=Nn[a]
            R=Nn
def factor_kernel(tokens,s_ref,g_ref,o_ref,A,X0,X1,G,Mh,Mm,Yh,Ym,MG):
    eye=jnp.where(lax.broadcasted_iota(jnp.int32,(B,B),0)==lax.broadcasted_iota(jnp.int32,(B,B),1),1.0,0.0).astype(F32)
    scale=1.0/tokens
    Xs=(X0,X1)
    def cov(r,n): return s_ref[r:r+n,:]*scale
    X0[...]=cov(0,B)+eye
    def start(g):
        rows=G.shape[0]//16
        for i in (2*g,2*g+1): G[i*rows:(i+1)*rows,:]=g_ref[i].astype(F32)[:rows,:]
    hook=start
    for j in range(8):
        X,Xn=Xs[j%2],Xs[1-j%2]
        inv128_h(X,hook)
        R=(7-j)*B; c=block_rows(j,j)+B
        dcat=rform3(X[...])
        jobs=[]
        if R:
            col=cov(c,R) if j==0 else A[c:c+R,:]
            ccat=lform3(col)
            m1=rform3(nt(ccat[0:B],dcat))
            rk=block_rows(j+1,j+1)
            old=(cov(rk,B)+eye) if j==0 else A[rk:rk+B,:]
            Xn[...]=old-nt(m1,ccat[0:B])
            st={}
            def j0(j=j,R=R,c=c,ccat=ccat,dcat=dcat,m1=m1,st=st):
                mcat=m1 if R==B else jnp.concatenate([m1,rform3(nt(ccat[B:R],dcat))],axis=0)
                st['m']=mcat
                Mh[c:c+R,:]=mcat[:,0:B]; Mm[c:c+R,:]=mcat[:,B:2*B]
            def j1(j=j,R=R,ccat=ccat,dcat=dcat,st=st):
                mg=nt(lform3(G[:,j*B:(j+1)*B]),dcat)
                MG[:,j*B:(j+1)*B]=mg
                st['g']=rform3(mg)
            jobs=[j0,j1]
            def tr(k,j=j,R=R,ccat=ccat,st=st):
                o=(k-j-1)*B; rk=block_rows(k,k); n=(8-k)*B
                if k==j+1: o2,rk,n=o+B,rk+B,n-B
                else: o2=o
                if n:
                    u=nt(st['m'][o2:R],ccat[o:o+B])
                    if j==0:
                        v=cov(rk,n)-u
                        if k!=j+1:
                            A[rk:rk+B,:]=v[0:B]+eye
                            if n>B: A[rk+B:rk+n,:]=v[B:]
                        else: A[rk:rk+n,:]=v
                    else: A[rk:rk+n,:]-=u
            def gu(lo,hi,j=j,ccat=ccat,st=st):
                if hi>lo: G[:,(j+1)*B+lo*B:(j+1)*B+hi*B]-=nt(st['g'],ccat[lo*B:hi*B])
            nk=7-j
            for k in range(j+1,8): jobs.append(functools.partial(tr,k))
            jobs.append(functools.partial(gu,0,nk//2)); jobs.append(functools.partial(gu,nk//2,nk))
        else:
            MG[:,j*B:]=nt(lform3(G[:,j*B:]),dcat)
        per=[[] for _ in range(8)]
        for i,jb in enumerate(jobs): per[min(7,i*8//max(1,len(jobs)))].append(jb)
        def hook(g,per=per):
            for jb in per[g]: jb()
    for j in range(7,-1,-1):
        y=MG[:,j*B:(j+1)*B]
        if j<7:
            c=block_rows(j,j)+B; R=(7-j)*B
            yh,ym=Yh[:,(j+1)*B:],Ym[:,(j+1)*B:]
            mh,mm=Mh[c:c+R,:],Mm[c:c+R,:]
            y=y-(jnp.dot(yh,mh,preferred_element_type=F32)+jnp.dot(yh,mm,preferred_element_type=F32)+jnp.dot(ym,mh,preferred_element_type=F32))
        h=y.astype(BF16)
        Yh[:,j*B:(j+1)*B]=h
        Ym[:,j*B:(j+1)*B]=(y-h.astype(F32)).astype(BF16)
        o_ref[:,j*B:(j+1)*B]=h
def factor(s,g,rows,tokens):
    vm=pl.BlockSpec(memory_space=pltpu.VMEM)
    n=16*rows
    return pl.pallas_call(functools.partial(factor_kernel,tokens),
      out_shape=jax.ShapeDtypeStruct((n,1024),BF16),in_specs=[vm,vm],out_specs=vm,
      scratch_shapes=[pltpu.VMEM((4608,B),F32),pltpu.VMEM((B,B),F32),pltpu.VMEM((B,B),F32),pltpu.VMEM((n,1024),F32),pltpu.VMEM((4608,B),BF16),pltpu.VMEM((4608,B),BF16),
        pltpu.VMEM((n,1024),BF16),pltpu.VMEM((n,1024),BF16),pltpu.VMEM((n,1024),F32)],
      compiler_params=pltpu.CompilerParams(vmem_limit_bytes=28<<20))(s,g)


def per_device(activations, gradient, block_map):
    tokens = activations.shape[0] * lax.axis_size("bcast")
    rows = gradient.shape[0]
    part = covariance(activations[:, 0, :])
    chooser = (block_map[None, :] == jnp.arange(16, dtype=jnp.int32)[:, None]).astype(BF16)
    padded = jnp.pad(gradient, ((0, -rows % 16), (0, 0), (0, 0)))
    ordered = jnp.einsum("kj,rjb->krb", chooser, padded, preferred_element_type=F32).astype(BF16)
    total, tiles = exchange(part, ordered)
    return factor(total, tiles, rows, tokens)[:, None, :]


def solution(mesh):
    return jax.shard_map(
        per_device,
        mesh=mesh,
        in_specs=(P("bcast", "grad", None), P(("bcast", "grad"), None, None), P()),
        out_specs=P("bcast", "grad", None),
        check_vma=False,
    )
```

```python
import functools

import jax
import jax.numpy as jnp
from jax import lax
from jax.experimental import pallas as pl
from jax.experimental.pallas import tpu as pltpu
from jax.sharding import PartitionSpec as P

MESH = pl.DeviceIdType.MESH
F32, BF16 = jnp.float32, jnp.bfloat16
B = 128


def block_rows(i, j):
    return (j * 8 - j * (j - 1) // 2 + (i - j)) * B


def covariance_kernel(act_ref, out_ref):
    for j in range(8):
        column = act_ref[:, j * B : (j + 1) * B]
        part = lax.dot_general(
            act_ref[:, j * B :], column, (((0,), (0,)), ((), ())), preferred_element_type=F32
        )
        out_ref[pl.ds(block_rows(j, j), (8 - j) * B), :] = part


def exchange_body(part_ref, grad_ref, sum_ref, tile_ref, acc, from_core, from_x, za_plus, za_minus, zb_plus, zb_minus, xa,
                  s_sem, r_sem, own_sem):
    H = 1152
    CA, SA = 144, 72
    XB, CB = 576, 72
    me = lax.axis_index("bcast")
    column = lax.axis_index("grad")
    core, z, x = me % 2, (me // 2) % 8, me // 16

    def at(c, zz, xx):
        return {"bcast": xx * 16 + (zz % 8) * 2 + c}

    twin, up, down, across = at(1 - core, z, x), at(core, z + 1, x), at(core, z + 7, x), at(core, z, 1 - x)
    barrier = pltpu.get_barrier_semaphore()
    for peer in (twin, up, down, across):
        pl.semaphore_signal(barrier, inc=1, device_id=peer, device_id_type=MESH)
    for d in range(1, 16):
        pl.semaphore_signal(barrier, inc=1, device_id={"grad": (column + d) % 16}, device_id_type=MESH)
    pl.semaphore_wait(barrier, 19)

    sent = []

    def send(src, dst, to):
        n = len(sent)
        c = pltpu.make_async_remote_copy(src_ref=src, dst_ref=dst, send_sem=s_sem.at[n], recv_sem=r_sem.at[n],
                                         device_id=to, device_id_type=MESH)
        c.start()
        sent.append(c)
        return c

    def ds(start, n):
        return pl.ds(pl.multiple_of(start, 8), n)

    def a_rows(q, h=None):
        return ds((q % 8) * CA + (0 if h is None else h * SA), CA if h is None else SA)

    def b_rows(xx, q=None):
        return ds(H + xx * XB + (0 if q is None else (q % 8) * CB), XB if q is None else CB)

    def pa(c, q, h=None):
        return ds(c * H + (q % 8) * CA + (0 if h is None else h * SA), CA if h is None else SA)

    def pb(c, xx, q=None):
        return ds(2 * H + c * H + xx * XB + (0 if q is None else (q % 8) * CB), XB if q is None else CB)

    order = [4, 5, 3, 6, 2, 7, 1, 0]
    swap_a = {}

    def swap(d):
        swap_a[d] = send(part_ref.at[pa(1 - core, z + d)], from_core.at[a_rows(z + d)], twin)

    swap(4), swap(5)
    swap_b0 = send(part_ref.at[pb(1 - core, 1 - x)], from_core.at[b_rows(1 - x)], twin)
    for d in order[2:]:
        swap(d)
    swap_b1 = send(part_ref.at[pb(1 - core, x)], from_core.at[b_rows(x)], twin)

    def add_a(d):
        swap_a[d].wait_recv()
        acc[a_rows(z + d)] = part_ref[pa(core, z + d)] + from_core[a_rows(z + d)]

    def ring(buf, k, rows, to):
        return send(acc.at[rows], buf.at[k], to)

    add_a(4)
    ap = [send(acc.at[a_rows(z + 4, h)], za_plus.at[0, h], up) for h in (0, 1)]
    add_a(5)
    am = [send(acc.at[a_rows(z + 5, h)], za_minus.at[0, h], down) for h in (0, 1)]
    swap_b0.wait_recv()
    acc[b_rows(1 - x)] = part_ref[pb(core, 1 - x)] + from_core[b_rows(1 - x)]
    bx = {d: send(acc.at[b_rows(1 - x, z + d)], from_x.at[ds(((z + d) % 8) * CB, CB)], across) for d in order}
    for d in order[2:]:
        add_a(d)
    swap_b1.wait_recv()
    acc[b_rows(x)] = part_ref[pb(core, x)] + from_core[b_rows(x)]

    def step_a(s):
        nonlocal ap, am
        q = []
        for h in (0, 1):
            ap[h].wait_recv()
            acc[a_rows(z + 4 - s, h)] += za_plus[s - 1, h]
            if s < 4:
                q.append(send(acc.at[a_rows(z + 4 - s, h)], za_plus.at[s, h], up))
            else:
                q.append(send(acc.at[a_rows(z, h)], xa.at[h], across))
        ap = q
        if s < 4:
            q = []
            for h in (0, 1):
                am[h].wait_recv()
                acc[a_rows(z + 5 + s, h)] += za_minus[s - 1, h]
                if s < 3:
                    q.append(send(acc.at[a_rows(z + 5 + s, h)], za_minus.at[s, h], down))
            am = q

    def take_x(d):
        bx[d].wait_recv()
        acc[b_rows(x, z + d)] += from_x[ds(((z + d) % 8) * CB, CB)]

    bp = bm = None

    def step_b(s):
        nonlocal bp, bm
        if s < 4:
            take_x(4 - s)
        if s == 4:
            acc[b_rows(x, z)] += zb_plus_wait()
        else:
            if s:
                bp.wait_recv()
                acc[b_rows(x, z + 4 - s)] += zb_plus[s - 1]
            bp = send(acc.at[b_rows(x, z + 4 - s)], zb_plus.at[s], up)
        if s < 4:
            take_x((5 + s) % 8)
            if s:
                bm.wait_recv()
                acc[b_rows(x, z + 5 + s)] += zb_minus[s - 1]
            if s < 3:
                bm = send(acc.at[b_rows(x, z + 5 + s)], zb_minus.at[s], down)

    def zb_plus_wait():
        bp.wait_recv()
        return zb_plus[3]

    step_a(1)
    step_b(0)
    step_a(2)
    step_b(1)
    step_a(3)
    step_b(2)
    own = pltpu.make_async_copy(grad_ref.at[column], tile_ref.at[column], own_sem)
    own.start()
    tiles = []
    for d in range(1, 16):
        to = (column + d) % 16
        tiles.append(send(grad_ref.at[to], tile_ref.at[column], {"grad": to}))
    step_a(4)
    step_b(3)

    def same(rows, to):
        return send(sum_ref.at[rows], sum_ref.at[rows], to)

    twins, xs = [], []

    def b_out(q, plus, minus):
        r = pb(core, x, q)
        p = same(r, up) if plus else None
        m = same(r, down) if minus else None
        xs.append((same(r, across), q))
        twins.append(same(r, twin))
        return p, m

    across_a, ap, am = ap, [None, None], [None, None]
    for h in (0, 1):
        across_a[h].wait_recv()
        r = pa(core, z, h)
        sum_ref[r] = acc[a_rows(z, h)] + xa[h]
        ap[h], am[h] = same(r, up), same(r, down)
        twins.append(same(r, twin))
    step_b(4)
    sum_ref[pb(core, x, z)] = acc[b_rows(x, z)]
    bp, bm = b_out(z, True, True)

    def relay():
        c, q = xs.pop(0)
        c.wait_recv()
        twins.append(same(pb(core, 1 - x, q), twin))

    for s in range(1, 5):
        for h in (0, 1):
            ap[h].wait_recv()
            r = pa(core, z + 8 - s, h)
            if s < 4:
                ap[h] = same(r, up)
            twins.append(same(r, twin))
            if s < 4:
                am[h].wait_recv()
                r = pa(core, z + s, h)
                if s < 3:
                    am[h] = same(r, down)
                twins.append(same(r, twin))
        bp.wait_recv()
        bp, _ = b_out(z + 8 - s, s < 4, False)
        if s < 4:
            bm.wait_recv()
            _, bm = b_out(z + s, False, s < 3)
        relay()
        if s > 1:
            relay()
    relay()
    for c in twins:
        c.wait_recv()
    for c in tiles:
        c.wait_recv()
    for c in sent:
        c.wait_send()
    own.wait()


N_COPIES = 160


def exchange(part, grads):
    dma = pltpu.SemaphoreType.DMA
    vm = pl.BlockSpec(memory_space=pltpu.VMEM)
    return pl.pallas_call(
        exchange_body,
        out_shape=(jax.ShapeDtypeStruct((4608, B), F32), jax.ShapeDtypeStruct(grads.shape, BF16)),
        in_specs=[vm, vm],
        out_specs=(vm, vm),
        scratch_shapes=[
            pltpu.VMEM((2304, B), F32), pltpu.VMEM((2304, B), F32), pltpu.VMEM((576, B), F32),
            pltpu.VMEM((4, 2, 72, B), F32), pltpu.VMEM((3, 2, 72, B), F32),
            pltpu.VMEM((4, 72, B), F32), pltpu.VMEM((3, 72, B), F32), pltpu.VMEM((2, 72, B), F32),
            dma((N_COPIES,)), dma((N_COPIES,)), dma,
        ],
        compiler_params=pltpu.CompilerParams(collective_id=0, has_side_effects=True, vmem_limit_bytes=18 << 20),
    )(part, grads)


def covariance(act):
    vm = pl.BlockSpec(memory_space=pltpu.VMEM)
    return pl.pallas_call(
        covariance_kernel,
        out_shape=jax.ShapeDtypeStruct((4608, B), F32),
        in_specs=[vm], out_specs=vm,
        compiler_params=pltpu.CompilerParams(vmem_limit_bytes=20 << 20),
    )(act)


def lb(t, j):
    return jnp.broadcast_to(t[:, j : j + 1], (8, B))


def sb(t, r):
    return jnp.broadcast_to(t[r : r + 1, :], (8, B))


def tsum(xs):
    xs = list(xs)
    while len(xs) > 1:
        xs = [xs[i] + xs[i + 1] if i + 1 < len(xs) else xs[i] for i in range(0, len(xs), 2)]
    return xs[0]

NT=(((1,),(1,)),((),()))
def nt(a,b): return lax.dot_general(a,b,NT,preferred_element_type=F32)
def split2(x):
    h=x.astype(BF16); return h,(x-h.astype(F32)).astype(BF16)
def lform3(x):
    h,m=split2(x); return jnp.concatenate([h,h,m],axis=1)
def rform3(x):
    h,m=split2(x); return jnp.concatenate([h,m,h],axis=1)
def gj(L, R, sub):
    for j in range(16):
        u, r = j // 8, j % 8
        dinv = 1.0 / sb(L[u][j], r)
        isr = sub == r
        t = sb(R[u], r) * dinv
        for k in range(j + 1, 16):
            tk = sb(L[u][k], r) * dinv
            for a in range(2):
                y = L[a][k] - L[a][j] * tk
                L[a][k] = jnp.where(isr, tk, y) if a == u else y
        R = [R[a] - L[a][j] * t for a in range(2)]
        R[u] = jnp.where(isr, t, R[u])
    return R


def inv128_h(X_ref,hook=None,p=16):
    lane=lax.broadcasted_iota(jnp.int32,(8,128),1)
    sub=lax.broadcasted_iota(jnp.int32,(8,128),0)
    lane_all=lax.broadcasted_iota(jnp.int32,(128,128),1)
    nv=p//8; Gn=128//p
    R=[X_ref[8*a:8*a+8,:] for a in range(nv)]
    for g in range(Gn):
        base=g*p; n=(g+1)%Gn
        N=[X_ref[n*p+8*a:n*p+8*a+8,:] for a in range(nv)]
        ing=(lane>=base)&(lane<base+p)
        L=[[lb(R[a],base+j) for j in range(p)] for a in range(nv)]
        Rh=[jnp.where(ing,jnp.where(lane-base==sub+8*a,1.0,0.0),R[a]) for a in range(nv)]
        X=X_ref[...]
        h,m=split2(X)
        LH=jnp.concatenate([h,h,m],axis=1)
        if g<Gn-1: CN=[[lb(N[a],base+j) for j in range(p)] for a in range(nv)]
        if hook is not None: hook(g)
        T=gj(L,Rh,sub)
        Tc=jnp.concatenate(T,axis=0)
        if g<Gn-1:
            Ts=[sb(T[j//8],j%8) for j in range(p)]
            Nn=[jnp.where(ing,0.0,N[a])-tsum([CN[a][j]*Ts[j] for j in range(p)]) for a in range(nv)]
        th,tm=split2(Tc)
        def pad(t):
            parts=[]
            if base: parts.append(jnp.zeros((base,128),BF16))
            parts.append(t)
            if base+p<128: parts.append(jnp.zeros((128-base-p,128),BF16))
            return jnp.concatenate(parts,axis=0)
        th,tm=pad(th),pad(tm)
        U=jnp.dot(LH,jnp.concatenate([th,tm,th],axis=0),preferred_element_type=F32)
        inga=(lane_all>=base)&(lane_all<base+p)
        X_ref[...]=jnp.where(inga,0.0,X)-U
        X_ref[base:base+p,:]=Tc
        if g<Gn-1:
            for a in range(nv): X_ref[n*p+8*a:n*p+8*a+8,:]=Nn[a]
            R=Nn
def factor_kernel(tokens,s_ref,g_ref,o_ref,A,X0,X1,G,Mh,Mm,Yh,Ym,MG):
    eye=jnp.where(lax.broadcasted_iota(jnp.int32,(B,B),0)==lax.broadcasted_iota(jnp.int32,(B,B),1),1.0,0.0).astype(F32)
    scale=1.0/tokens
    Xs=(X0,X1)
    def cov(r,n): return s_ref[r:r+n,:]*scale
    X0[...]=cov(0,B)+eye
    def start(g):
        rows=G.shape[0]//16
        for i in (2*g,2*g+1): G[i*rows:(i+1)*rows,:]=g_ref[i].astype(F32)[:rows,:]
    hook=start
    for j in range(8):
        X,Xn=Xs[j%2],Xs[1-j%2]
        inv128_h(X,hook)
        R=(7-j)*B; c=block_rows(j,j)+B
        dcat=rform3(X[...])
        jobs=[]
        if R:
            col=cov(c,R) if j==0 else A[c:c+R,:]
            ccat=lform3(col)
            m1=rform3(nt(ccat[0:B],dcat))
            rk=block_rows(j+1,j+1)
            old=(cov(rk,B)+eye) if j==0 else A[rk:rk+B,:]
            Xn[...]=old-nt(m1,ccat[0:B])
            st={}
            def j0(j=j,R=R,c=c,ccat=ccat,dcat=dcat,m1=m1,st=st):
                mcat=m1 if R==B else jnp.concatenate([m1,rform3(nt(ccat[B:R],dcat))],axis=0)
                st['m']=mcat
                Mh[c:c+R,:]=mcat[:,0:B]; Mm[c:c+R,:]=mcat[:,B:2*B]
            def j1(j=j,R=R,ccat=ccat,dcat=dcat,st=st):
                mg=nt(lform3(G[:,j*B:(j+1)*B]),dcat)
                MG[:,j*B:(j+1)*B]=mg
                st['g']=rform3(mg)
            jobs=[j0,j1]
            def tr(k,j=j,R=R,ccat=ccat,st=st):
                o=(k-j-1)*B; rk=block_rows(k,k); n=(8-k)*B
                if k==j+1: o2,rk,n=o+B,rk+B,n-B
                else: o2=o
                if n:
                    u=nt(st['m'][o2:R],ccat[o:o+B])
                    if j==0:
                        v=cov(rk,n)-u
                        if k!=j+1:
                            A[rk:rk+B,:]=v[0:B]+eye
                            if n>B: A[rk+B:rk+n,:]=v[B:]
                        else: A[rk:rk+n,:]=v
                    else: A[rk:rk+n,:]-=u
            def gu(lo,hi,j=j,ccat=ccat,st=st):
                if hi>lo: G[:,(j+1)*B+lo*B:(j+1)*B+hi*B]-=nt(st['g'],ccat[lo*B:hi*B])
            nk=7-j
            for k in range(j+1,8): jobs.append(functools.partial(tr,k))
            jobs.append(functools.partial(gu,0,nk//2)); jobs.append(functools.partial(gu,nk//2,nk))
        else:
            MG[:,j*B:]=nt(lform3(G[:,j*B:]),dcat)
        per=[[] for _ in range(8)]
        for i,jb in enumerate(jobs): per[min(7,i*8//max(1,len(jobs)))].append(jb)
        def hook(g,per=per):
            for jb in per[g]: jb()
    for j in range(7,-1,-1):
        y=MG[:,j*B:(j+1)*B]
        if j<7:
            c=block_rows(j,j)+B; R=(7-j)*B
            yh,ym=Yh[:,(j+1)*B:],Ym[:,(j+1)*B:]
            mh,mm=Mh[c:c+R,:],Mm[c:c+R,:]
            y=y-(jnp.dot(yh,mh,preferred_element_type=F32)+jnp.dot(yh,mm,preferred_element_type=F32)+jnp.dot(ym,mh,preferred_element_type=F32))
        h=y.astype(BF16)
        Yh[:,j*B:(j+1)*B]=h
        Ym[:,j*B:(j+1)*B]=(y-h.astype(F32)).astype(BF16)
        o_ref[:,j*B:(j+1)*B]=h
def factor(s,g,rows,tokens):
    vm=pl.BlockSpec(memory_space=pltpu.VMEM)
    n=16*rows
    return pl.pallas_call(functools.partial(factor_kernel,tokens),
      out_shape=jax.ShapeDtypeStruct((n,1024),BF16),in_specs=[vm,vm],out_specs=vm,
      scratch_shapes=[pltpu.VMEM((4608,B),F32),pltpu.VMEM((B,B),F32),pltpu.VMEM((B,B),F32),pltpu.VMEM((n,1024),F32),pltpu.VMEM((4608,B),BF16),pltpu.VMEM((4608,B),BF16),
        pltpu.VMEM((n,1024),BF16),pltpu.VMEM((n,1024),BF16),pltpu.VMEM((n,1024),F32)],
      compiler_params=pltpu.CompilerParams(vmem_limit_bytes=28<<20))(s,g)


def per_device(activations, gradient, block_map):
    tokens = activations.shape[0] * lax.axis_size("bcast")
    rows = gradient.shape[0]
    part = covariance(activations[:, 0, :])
    chooser = (block_map[None, :] == jnp.arange(16, dtype=jnp.int32)[:, None]).astype(BF16)
    padded = jnp.pad(gradient, ((0, -rows % 16), (0, 0), (0, 0)))
    ordered = jnp.einsum("kj,rjb->krb", chooser, padded, preferred_element_type=F32).astype(BF16)
    total, tiles = exchange(part, ordered)
    return factor(total, tiles, rows, tokens)[:, None, :]


def solution(mesh):
    return jax.shard_map(
        per_device,
        mesh=mesh,
        in_specs=(P("bcast", "grad", None), P(("bcast", "grad"), None, None), P()),
        out_specs=P("bcast", "grad", None),
        check_vma=False,
    )
```

```python
import functools

import jax
import jax.numpy as jnp
from jax import lax
from jax.experimental import pallas as pl
from jax.experimental.pallas import tpu as pltpu
from jax.sharding import PartitionSpec as P

MESH = pl.DeviceIdType.MESH
F32, BF16 = jnp.float32, jnp.bfloat16
B = 128


def block_rows(i, j):
    return (j * 8 - j * (j - 1) // 2 + (i - j)) * B


def covariance_kernel(act_ref, out_ref):
    for j in range(0, 8, 2):
        columns = act_ref[:, j * B : (j + 2) * B]
        part = lax.dot_general(
            act_ref[:, j * B :], columns, (((0,), (0,)), ((), ())), preferred_element_type=F32
        )
        n = (8 - j) * B
        out_ref[pl.ds(block_rows(j, j), n), :] = part[:, :B]
        out_ref[pl.ds(block_rows(j + 1, j + 1), n - B), :] = part[B:, B:]


def exchange_body(part_ref, grad_ref, sum_ref, tile_ref, acc, from_core, from_x, za_plus, za_minus, zb_plus, zb_minus, xa,
                  s_sem, r_sem, own_sem):
    H = 1152
    CA, SA = 144, 72
    XB, CB = 576, 72
    me = lax.axis_index("bcast")
    column = lax.axis_index("grad")
    core, z, x = me % 2, (me // 2) % 8, me // 16

    def at(c, zz, xx):
        return {"bcast": xx * 16 + (zz % 8) * 2 + c}

    twin, up, down, across = at(1 - core, z, x), at(core, z + 1, x), at(core, z + 7, x), at(core, z, 1 - x)
    barrier = pltpu.get_barrier_semaphore()
    for peer in (twin, up, down, across):
        pl.semaphore_signal(barrier, inc=1, device_id=peer, device_id_type=MESH)
    for d in range(1, 16):
        pl.semaphore_signal(barrier, inc=1, device_id={"grad": (column + d) % 16}, device_id_type=MESH)
    pl.semaphore_wait(barrier, 19)

    sent = []

    def send(src, dst, to):
        n = len(sent)
        c = pltpu.make_async_remote_copy(src_ref=src, dst_ref=dst, send_sem=s_sem.at[n], recv_sem=r_sem.at[n],
                                         device_id=to, device_id_type=MESH)
        c.start()
        sent.append(c)
        return c

    def ds(start, n):
        return pl.ds(pl.multiple_of(start, 8), n)

    def a_rows(q, h=None):
        return ds((q % 8) * CA + (0 if h is None else h * SA), CA if h is None else SA)

    def b_rows(xx, q=None):
        return ds(H + xx * XB + (0 if q is None else (q % 8) * CB), XB if q is None else CB)

    def pa(c, q, h=None):
        return ds(c * H + (q % 8) * CA + (0 if h is None else h * SA), CA if h is None else SA)

    def pb(c, xx, q=None):
        return ds(2 * H + c * H + xx * XB + (0 if q is None else (q % 8) * CB), XB if q is None else CB)

    order = [4, 5, 3, 6, 2, 7, 1, 0]
    swap_a = {}

    def swap(d):
        swap_a[d] = send(part_ref.at[pa(1 - core, z + d)], from_core.at[a_rows(z + d)], twin)

    swap(4), swap(5)
    swap_b0 = send(part_ref.at[pb(1 - core, 1 - x)], from_core.at[b_rows(1 - x)], twin)
    for d in order[2:]:
        swap(d)
    swap_b1 = send(part_ref.at[pb(1 - core, x)], from_core.at[b_rows(x)], twin)

    def add_a(d):
        swap_a[d].wait_recv()
        acc[a_rows(z + d)] = part_ref[pa(core, z + d)] + from_core[a_rows(z + d)]

    def ring(buf, k, rows, to):
        return send(acc.at[rows], buf.at[k], to)

    add_a(4)
    ap = [send(acc.at[a_rows(z + 4, h)], za_plus.at[0, h], up) for h in (0, 1)]
    add_a(5)
    am = [send(acc.at[a_rows(z + 5, h)], za_minus.at[0, h], down) for h in (0, 1)]
    swap_b0.wait_recv()
    acc[b_rows(1 - x)] = part_ref[pb(core, 1 - x)] + from_core[b_rows(1 - x)]
    bx = {d: send(acc.at[b_rows(1 - x, z + d)], from_x.at[ds(((z + d) % 8) * CB, CB)], across) for d in order}
    for d in order[2:]:
        add_a(d)
    swap_b1.wait_recv()
    acc[b_rows(x)] = part_ref[pb(core, x)] + from_core[b_rows(x)]

    def step_a(s):
        nonlocal ap, am
        q = []
        for h in (0, 1):
            ap[h].wait_recv()
            acc[a_rows(z + 4 - s, h)] += za_plus[s - 1, h]
            if s < 4:
                q.append(send(acc.at[a_rows(z + 4 - s, h)], za_plus.at[s, h], up))
            else:
                q.append(send(acc.at[a_rows(z, h)], xa.at[h], across))
        ap = q
        if s < 4:
            q = []
            for h in (0, 1):
                am[h].wait_recv()
                acc[a_rows(z + 5 + s, h)] += za_minus[s - 1, h]
                if s < 3:
                    q.append(send(acc.at[a_rows(z + 5 + s, h)], za_minus.at[s, h], down))
            am = q

    def take_x(d):
        bx[d].wait_recv()
        acc[b_rows(x, z + d)] += from_x[ds(((z + d) % 8) * CB, CB)]

    bp = bm = None

    def step_b(s):
        nonlocal bp, bm
        if s < 4:
            take_x(4 - s)
        if s == 4:
            acc[b_rows(x, z)] += zb_plus_wait()
        else:
            if s:
                bp.wait_recv()
                acc[b_rows(x, z + 4 - s)] += zb_plus[s - 1]
            bp = send(acc.at[b_rows(x, z + 4 - s)], zb_plus.at[s], up)
        if s < 4:
            take_x((5 + s) % 8)
            if s:
                bm.wait_recv()
                acc[b_rows(x, z + 5 + s)] += zb_minus[s - 1]
            if s < 3:
                bm = send(acc.at[b_rows(x, z + 5 + s)], zb_minus.at[s], down)

    def zb_plus_wait():
        bp.wait_recv()
        return zb_plus[3]

    step_a(1)
    step_b(0)
    step_a(2)
    step_b(1)
    step_a(3)
    step_b(2)
    own = pltpu.make_async_copy(grad_ref.at[column], tile_ref.at[column], own_sem)
    own.start()
    tiles = []
    for d in range(1, 16):
        to = (column + d) % 16
        tiles.append(send(grad_ref.at[to], tile_ref.at[column], {"grad": to}))
    step_a(4)
    step_b(3)

    def same(rows, to):
        return send(sum_ref.at[rows], sum_ref.at[rows], to)

    twins, xs = [], []

    def b_out(q, plus, minus):
        r = pb(core, x, q)
        p = same(r, up) if plus else None
        m = same(r, down) if minus else None
        xs.append((same(r, across), q))
        twins.append(same(r, twin))
        return p, m

    across_a, ap, am = ap, [None, None], [None, None]
    for h in (0, 1):
        across_a[h].wait_recv()
        r = pa(core, z, h)
        sum_ref[r] = acc[a_rows(z, h)] + xa[h]
        ap[h], am[h] = same(r, up), same(r, down)
        twins.append(same(r, twin))
    step_b(4)
    sum_ref[pb(core, x, z)] = acc[b_rows(x, z)]
    bp, bm = b_out(z, True, True)

    def relay():
        c, q = xs.pop(0)
        c.wait_recv()
        twins.append(same(pb(core, 1 - x, q), twin))

    for s in range(1, 5):
        for h in (0, 1):
            ap[h].wait_recv()
            r = pa(core, z + 8 - s, h)
            if s < 4:
                ap[h] = same(r, up)
            twins.append(same(r, twin))
            if s < 4:
                am[h].wait_recv()
                r = pa(core, z + s, h)
                if s < 3:
                    am[h] = same(r, down)
                twins.append(same(r, twin))
        bp.wait_recv()
        bp, _ = b_out(z + 8 - s, s < 4, False)
        if s < 4:
            bm.wait_recv()
            _, bm = b_out(z + s, False, s < 3)
        relay()
        if s > 1:
            relay()
    relay()
    for c in twins:
        c.wait_recv()
    for c in tiles:
        c.wait_recv()
    for c in sent:
        c.wait_send()
    own.wait()


N_COPIES = 160


def exchange(part, grads):
    dma = pltpu.SemaphoreType.DMA
    vm = pl.BlockSpec(memory_space=pltpu.VMEM)
    return pl.pallas_call(
        exchange_body,
        out_shape=(jax.ShapeDtypeStruct((4608, B), F32), jax.ShapeDtypeStruct(grads.shape, BF16)),
        in_specs=[vm, vm],
        out_specs=(vm, vm),
        scratch_shapes=[
            pltpu.VMEM((2304, B), F32), pltpu.VMEM((2304, B), F32), pltpu.VMEM((576, B), F32),
            pltpu.VMEM((4, 2, 72, B), F32), pltpu.VMEM((3, 2, 72, B), F32),
            pltpu.VMEM((4, 72, B), F32), pltpu.VMEM((3, 72, B), F32), pltpu.VMEM((2, 72, B), F32),
            dma((N_COPIES,)), dma((N_COPIES,)), dma,
        ],
        compiler_params=pltpu.CompilerParams(collective_id=0, has_side_effects=True, vmem_limit_bytes=18 << 20),
    )(part, grads)


def covariance(act):
    vm = pl.BlockSpec(memory_space=pltpu.VMEM)
    return pl.pallas_call(
        covariance_kernel,
        out_shape=jax.ShapeDtypeStruct((4608, B), F32),
        in_specs=[vm], out_specs=vm,
        compiler_params=pltpu.CompilerParams(vmem_limit_bytes=20 << 20),
    )(act)


def lb(t, j):
    return jnp.broadcast_to(t[:, j : j + 1], (8, B))


def sb(t, r):
    return jnp.broadcast_to(t[r : r + 1, :], (8, B))


def tsum(xs):
    xs = list(xs)
    while len(xs) > 1:
        xs = [xs[i] + xs[i + 1] if i + 1 < len(xs) else xs[i] for i in range(0, len(xs), 2)]
    return xs[0]

NT=(((1,),(1,)),((),()))
def nt(a,b): return lax.dot_general(a,b,NT,preferred_element_type=F32)
def split2(x):
    h=x.astype(BF16); return h,(x-h.astype(F32)).astype(BF16)
def lform3(x):
    h,m=split2(x); return jnp.concatenate([h,h,m],axis=1)
def rform3(x):
    h,m=split2(x); return jnp.concatenate([h,m,h],axis=1)
def gj(L, R, sub):
    for j in range(16):
        u, r = j // 8, j % 8
        dinv = 1.0 / sb(L[u][j], r)
        isr = sub == r
        t = sb(R[u], r) * dinv
        for k in range(j + 1, 16):
            tk = sb(L[u][k], r) * dinv
            for a in range(2):
                y = L[a][k] - L[a][j] * tk
                L[a][k] = jnp.where(isr, tk, y) if a == u else y
        R = [R[a] - L[a][j] * t for a in range(2)]
        R[u] = jnp.where(isr, t, R[u])
    return R


def inv128_h(X_ref,hook=None,p=16):
    lane=lax.broadcasted_iota(jnp.int32,(8,128),1)
    sub=lax.broadcasted_iota(jnp.int32,(8,128),0)
    lane_all=lax.broadcasted_iota(jnp.int32,(128,128),1)
    nv=p//8; Gn=128//p
    R=[X_ref[8*a:8*a+8,:] for a in range(nv)]
    for g in range(Gn):
        base=g*p; n=(g+1)%Gn
        N=[X_ref[n*p+8*a:n*p+8*a+8,:] for a in range(nv)]
        ing=(lane>=base)&(lane<base+p)
        L=[[lb(R[a],base+j) for j in range(p)] for a in range(nv)]
        Rh=[jnp.where(ing,jnp.where(lane-base==sub+8*a,1.0,0.0),R[a]) for a in range(nv)]
        X=X_ref[...]
        h,m=split2(X)
        LH=jnp.concatenate([h,h,m],axis=1)
        if g<Gn-1: CN=[[lb(N[a],base+j) for j in range(p)] for a in range(nv)]
        if hook is not None: hook(g)
        T=gj(L,Rh,sub)
        Tc=jnp.concatenate(T,axis=0)
        if g<Gn-1:
            Ts=[sb(T[j//8],j%8) for j in range(p)]
            Nn=[jnp.where(ing,0.0,N[a])-tsum([CN[a][j]*Ts[j] for j in range(p)]) for a in range(nv)]
        th,tm=split2(Tc)
        def pad(t):
            parts=[]
            if base: parts.append(jnp.zeros((base,128),BF16))
            parts.append(t)
            if base+p<128: parts.append(jnp.zeros((128-base-p,128),BF16))
            return jnp.concatenate(parts,axis=0)
        th,tm=pad(th),pad(tm)
        U=jnp.dot(LH,jnp.concatenate([th,tm,th],axis=0),preferred_element_type=F32)
        inga=(lane_all>=base)&(lane_all<base+p)
        X_ref[...]=jnp.where(inga,0.0,X)-U
        X_ref[base:base+p,:]=Tc
        if g<Gn-1:
            for a in range(nv): X_ref[n*p+8*a:n*p+8*a+8,:]=Nn[a]
            R=Nn
def factor_kernel(tokens,s_ref,g_ref,o_ref,A,X0,X1,G,Mh,Mm,Yh,Ym,MG):
    eye=jnp.where(lax.broadcasted_iota(jnp.int32,(B,B),0)==lax.broadcasted_iota(jnp.int32,(B,B),1),1.0,0.0).astype(F32)
    scale=1.0/tokens
    Xs=(X0,X1)
    def cov(r,n): return s_ref[r:r+n,:]*scale
    X0[...]=cov(0,B)+eye
    def start(g):
        rows=G.shape[0]//16
        for i in (2*g,2*g+1): G[i*rows:(i+1)*rows,:]=g_ref[i].astype(F32)[:rows,:]
    hook=start
    for j in range(8):
        X,Xn=Xs[j%2],Xs[1-j%2]
        inv128_h(X,hook)
        R=(7-j)*B; c=block_rows(j,j)+B
        dcat=rform3(X[...])
        jobs=[]
        if R:
            col=cov(c,R) if j==0 else A[c:c+R,:]
            ccat=lform3(col)
            m1=rform3(nt(ccat[0:B],dcat))
            rk=block_rows(j+1,j+1)
            old=(cov(rk,B)+eye) if j==0 else A[rk:rk+B,:]
            Xn[...]=old-nt(m1,ccat[0:B])
            st={}
            def j0(j=j,R=R,c=c,ccat=ccat,dcat=dcat,m1=m1,st=st):
                mcat=m1 if R==B else jnp.concatenate([m1,rform3(nt(ccat[B:R],dcat))],axis=0)
                st['m']=mcat
                Mh[c:c+R,:]=mcat[:,0:B]; Mm[c:c+R,:]=mcat[:,B:2*B]
            def j1(j=j,R=R,ccat=ccat,dcat=dcat,st=st):
                mg=nt(lform3(G[:,j*B:(j+1)*B]),dcat)
                MG[:,j*B:(j+1)*B]=mg
                st['g']=rform3(mg)
            jobs=[j0,j1]
            def tr(k,j=j,R=R,ccat=ccat,st=st):
                o=(k-j-1)*B; rk=block_rows(k,k); n=(8-k)*B
                if k==j+1: o2,rk,n=o+B,rk+B,n-B
                else: o2=o
                if n:
                    u=nt(st['m'][o2:R],ccat[o:o+B])
                    if j==0:
                        v=cov(rk,n)-u
                        if k!=j+1:
                            A[rk:rk+B,:]=v[0:B]+eye
                            if n>B: A[rk+B:rk+n,:]=v[B:]
                        else: A[rk:rk+n,:]=v
                    else: A[rk:rk+n,:]-=u
            def gu(lo,hi,j=j,ccat=ccat,st=st):
                if hi>lo: G[:,(j+1)*B+lo*B:(j+1)*B+hi*B]-=nt(st['g'],ccat[lo*B:hi*B])
            nk=7-j
            for k in range(j+1,8): jobs.append(functools.partial(tr,k))
            jobs.append(functools.partial(gu,0,nk//2)); jobs.append(functools.partial(gu,nk//2,nk))
        else:
            MG[:,j*B:]=nt(lform3(G[:,j*B:]),dcat)
        per=[[] for _ in range(8)]
        for i,jb in enumerate(jobs): per[min(7,i*8//max(1,len(jobs)))].append(jb)
        def hook(g,per=per):
            for jb in per[g]: jb()
    for j in range(7,-1,-1):
        y=MG[:,j*B:(j+1)*B]
        if j<7:
            c=block_rows(j,j)+B; R=(7-j)*B
            yh,ym=Yh[:,(j+1)*B:],Ym[:,(j+1)*B:]
            mh,mm=Mh[c:c+R,:],Mm[c:c+R,:]
            y=y-(jnp.dot(yh,mh,preferred_element_type=F32)+jnp.dot(yh,mm,preferred_element_type=F32)+jnp.dot(ym,mh,preferred_element_type=F32))
        h=y.astype(BF16)
        Yh[:,j*B:(j+1)*B]=h
        Ym[:,j*B:(j+1)*B]=(y-h.astype(F32)).astype(BF16)
        o_ref[:,j*B:(j+1)*B]=h
def factor(s,g,rows,tokens):
    vm=pl.BlockSpec(memory_space=pltpu.VMEM)
    n=16*rows
    return pl.pallas_call(functools.partial(factor_kernel,tokens),
      out_shape=jax.ShapeDtypeStruct((n,1024),BF16),in_specs=[vm,vm],out_specs=vm,
      scratch_shapes=[pltpu.VMEM((4608,B),F32),pltpu.VMEM((B,B),F32),pltpu.VMEM((B,B),F32),pltpu.VMEM((n,1024),F32),pltpu.VMEM((4608,B),BF16),pltpu.VMEM((4608,B),BF16),
        pltpu.VMEM((n,1024),BF16),pltpu.VMEM((n,1024),BF16),pltpu.VMEM((n,1024),F32)],
      compiler_params=pltpu.CompilerParams(vmem_limit_bytes=28<<20))(s,g)


def per_device(activations, gradient, block_map):
    tokens = activations.shape[0] * lax.axis_size("bcast")
    rows = gradient.shape[0]
    part = covariance(activations[:, 0, :])
    chooser = (block_map[None, :] == jnp.arange(16, dtype=jnp.int32)[:, None]).astype(BF16)
    padded = jnp.pad(gradient, ((0, -rows % 16), (0, 0), (0, 0)))
    ordered = jnp.einsum("kj,rjb->krb", chooser, padded, preferred_element_type=F32).astype(BF16)
    total, tiles = exchange(part, ordered)
    return factor(total, tiles, rows, tokens)[:, None, :]


def solution(mesh):
    return jax.shard_map(
        per_device,
        mesh=mesh,
        in_specs=(P("bcast", "grad", None), P(("bcast", "grad"), None, None), P()),
        out_specs=P("bcast", "grad", None),
        check_vma=False,
    )
```
